256 devices in a mesh: seq: 8 (over z), ctx: 32 (over y, x, core).
Axes of the slice: x: 4, y: 4, z: 8, core: 2. Of those that a mesh axis runs over, the one named last changes fastest.
Arguments:
- inputs: bfloat16 [65536, 2048], P(('seq', 'ctx')), parts along dimension 0, may hold values from -0.19921875 to 0.19921875
- write_keys: bfloat16 [65536, 128], P(('seq', 'ctx')), parts along dimension 0, may hold values from -0.5 to 0.5
- read_queries: bfloat16 [65536, 128], P(('seq', 'ctx')), parts along dimension 0, may hold values from -6 to 6
- decay_log: float32 [32, 65536], P(None, ('seq', 'ctx')), parts along dimension 1, may hold values from -1 to 0
- level_mix: float32 [6, 32, 65536], P(None, None, ('seq', 'ctx')), parts along dimension 2, may hold values from 0.25 to 1.5
Outputs:
- outputs: bfloat16 [65536, 2048], P(('seq', 'ctx')), parts along dimension 0
The draws below stay inside these ranges and needn't reach their ends.
There are 8 independent parts, one for each index of `seq`. The reference program is written for one: setup_inputs(seed, part) draws one part's arguments, and reference() takes and returns one part's arrays. A program takes and returns all parts, laid end to end along the dimension named above; each array names one. Nothing has to cross between parts.
All inputs are finite; a program needn't handle non-finite values.
Results may differ from the reference program's by a relative error of at most 0.0062.
Values may be sent and summed in bfloat16 or wider, within the bound.
No kernel may reach another device: no remote copies, remote signals or barrier semaphores. Data moves between devices by JAX's collectives and lax.ppermute only.
A program may use at most 128 MiB of HBM per device.

```python
import math
import jax
import jax.numpy as jnp
from jax import lax

HEADS = 32
HEAD = 64
STATE = 128
TOK_DEV = 256
SUB = 256
LEVELS = 5
TOKENS = 8192


def draw_decay_log(key, part):
    key = jax.random.fold_in(key, 11)
    keys_split = jax.random.split(key, 7)
    quick_fraction = 0.5
    fast = jax.random.uniform(keys_split[0], (HEADS,)) < quick_fraction
    slow_rate = jnp.exp(jax.random.uniform(keys_split[1], (HEADS,), minval=math.log(0.05), maxval=math.log(0.3))) / TOKENS
    fast_rate = jax.random.uniform(keys_split[2], (HEADS,), minval=1.0 / 50.0, maxval=1.0 / 30.0)
    decay_speed = jnp.where(fast, fast_rate, slow_rate)
    block_multiplier = jnp.repeat(jnp.exp(jax.random.uniform(keys_split[3], (TOKENS // TOK_DEV,), minval=-0.7, maxval=0.7)), TOK_DEV)
    token_multiplier = jnp.exp(jax.random.uniform(keys_split[4], (HEADS, TOKENS), minval=-0.7, maxval=0.7))
    positions = jax.random.randint(keys_split[5], (3,), 0, TOKENS)
    level_depth = jax.random.uniform(keys_split[6], (3,), minval=0.2, maxval=0.5)
    token_locations = jnp.arange(TOKENS)[None, :] == positions[:, None]
    spike_amount = jnp.sum(jnp.where(token_locations, jnp.log(1.0 - level_depth)[:, None], 0.0), axis=0)
    return (-(decay_speed[:, None] * block_multiplier[None, :] * token_multiplier) + spike_amount[None, :]).astype(jnp.float32)


def levels(key, extent, shards, least, top_value):
    factor_of = 1.0
    for dim, blocks in shards:
        heights = jax.random.uniform(jax.random.fold_in(jax.random.fold_in(key, 6), dim), (blocks,), jnp.float32, least / len(shards), top_value / len(shards))
        factor_of = factor_of * jnp.repeat(jnp.exp(heights), extent[dim] // blocks).reshape((-1,) + (1,) * (len(extent) - 1 - dim))
    return factor_of


def scatter_about(stream_key, extent, spread, bound, shards=(), kind=jnp.bfloat16):
    gain = levels(stream_key, extent, shards, -0.22, 0.18) if shards else 1.0
    drawn = jax.random.normal(stream_key, extent, jnp.float32) * spread * gain
    return jnp.minimum(jnp.maximum(drawn, -bound), bound).astype(kind)


def setup_inputs(seed: int = 0, part: int = 0) -> dict:
    splits = jax.random.split(jax.random.key(seed), 6)
    part_keys = jax.random.split(jax.random.fold_in(splits[5], part), 6)
    return {
        "inputs": scatter_about(part_keys[0], (TOKENS, HEADS * HEAD), 0.03, 0.19921875, ((0, 32),)),
        "write_keys": scatter_about(part_keys[1], (TOKENS, STATE), STATE ** -0.5, 0.5, ((0, 32),)),
        "read_queries": scatter_about(part_keys[2], (TOKENS, STATE), 1.0, 6.0, ((0, 32),)),
        "decay_log": draw_decay_log(jax.random.fold_in(jax.random.fold_in(splits[5], part), 71), part),
        "level_mix": jnp.clip(0.25 + 1.25 * jax.random.uniform(part_keys[4], (LEVELS + 1, HEADS, TOKENS), jnp.float32) ** levels(part_keys[4], (LEVELS + 1, HEADS, TOKENS), ((2, 32),), -0.2, 0.2), 0.25, 1.5),
    }


def level_mask(reader, source, level):
    reader_bit = (reader >> level) & 1
    source_bit = (source >> level) & 1
    same_high = (reader >> (level + 1)) == (source >> (level + 1))
    return (reader_bit == 1) & (source_bit == 0) & same_high


def local_block(x_block, key_block, query_block, decay_block):
    length = x_block.shape[0]
    head_count = x_block.shape[1]
    pieces = length // SUB
    x_parts = x_block.reshape(pieces, SUB, head_count, HEAD)
    key_parts = key_block.reshape(pieces, SUB, key_block.shape[1])
    query_parts = query_block.reshape(pieces, SUB, query_block.shape[1])
    decay_parts = decay_block.reshape(head_count, pieces, SUB).transpose(1, 0, 2)
    causal = jnp.arange(SUB)[:, None] >= jnp.arange(SUB)[None, :]

    def step(carry, piece):
        state, offset = carry
        x_sub, key_sub, query_sub, decay_sub = piece
        cum = jnp.cumsum(decay_sub, axis=1)
        scores = jnp.dot(query_sub, key_sub.T, preferred_element_type=jnp.float32)
        gap = cum[:, :, None] - cum[:, None, :]
        mixing = jnp.where(causal[None], scores[None] * jnp.exp(jnp.where(causal[None], gap, 0.0)), 0.0)
        mixing = lax.optimization_barrier(mixing.astype(jnp.bfloat16)).astype(jnp.float32)
        diagonal = jnp.einsum("hts,shp->thp", mixing, x_sub.astype(jnp.float32))
        rounded = lax.optimization_barrier(state.astype(jnp.bfloat16)).astype(jnp.float32)
        carried = jnp.einsum("tn,hnp->thp", query_sub.astype(jnp.float32), rounded)
        local = diagonal + jnp.exp(cum).T[:, :, None] * carried
        factor = jnp.exp(cum[:, -1:] - cum)
        decayed = (x_sub.astype(jnp.float32) * factor.T[:, :, None]).astype(jnp.bfloat16)
        decayed = lax.optimization_barrier(decayed).astype(jnp.float32)
        update = jnp.einsum("sn,shp->hnp", key_sub.astype(jnp.float32), decayed)
        state = jnp.exp(cum[:, -1])[:, None, None] * state + update
        within = cum + offset[:, None]
        offset = offset + cum[:, -1]
        return (state, offset), (local, within)

    start = (jnp.zeros((head_count, key_block.shape[1], HEAD), jnp.float32), jnp.zeros((head_count,), jnp.float32))
    (state, offset), (local, within) = lax.scan(step, start, (x_parts, key_parts, query_parts, decay_parts))
    local = local.reshape(length, head_count, HEAD)
    within = within.transpose(1, 0, 2).reshape(head_count, length)
    return local, state, offset, within


def reference(inputs, write_keys, read_queries, decay_log, level_mix):
    blocks = TOKENS // TOK_DEV
    x_all = inputs.reshape(blocks, TOK_DEV, HEADS, HEAD)
    key_all = write_keys.reshape(blocks, TOK_DEV, STATE)
    query_all = read_queries.reshape(blocks, TOK_DEV, STATE)
    decay_all = decay_log.reshape(HEADS, blocks, TOK_DEV).transpose(1, 0, 2)
    mix_all = level_mix.reshape(LEVELS + 1, HEADS, blocks, TOK_DEV).transpose(2, 0, 1, 3)
    local, ends, totals, within = lax.map(lambda group: local_block(*group), (x_all, key_all, query_all, decay_all))
    ends = lax.optimization_barrier(ends.astype(jnp.bfloat16)).astype(jnp.float32)
    inclusive = jnp.cumsum(totals, axis=0)
    exclusive = inclusive - totals
    sources = jnp.arange(blocks, dtype=jnp.int32)

    def reader(group):
        reader_id, queries, mixes, local_part, within_part = group
        total = mixes[0].T[:, :, None] * local_part
        scale = jnp.exp(within_part).T
        gap = exclusive[reader_id][None, :] - inclusive
        for level in range(LEVELS):
            chosen = level_mask(reader_id, sources, level)[:, None]
            weights = jnp.where(chosen, jnp.exp(jnp.where(chosen, gap, 0.0)), 0.0)
            merged = jnp.einsum("kh,khnp->hnp", weights, ends, precision=lax.Precision.HIGHEST)
            rounded = lax.optimization_barrier(merged.astype(jnp.bfloat16)).astype(jnp.float32)
            product = jnp.einsum("tn,hnp->thp", queries.astype(jnp.float32), rounded)
            total = total + (mixes[level + 1].T * scale)[:, :, None] * product
        return total.astype(jnp.bfloat16).reshape(TOK_DEV, HEADS * HEAD)

    result = lax.map(reader, (sources, query_all, mix_all, local, within))
    return result.reshape(TOKENS, HEADS * HEAD)
```

```python
import functools

import jax
import jax.numpy as jnp
from jax import lax
from jax.experimental import pallas as pl
from jax.experimental.pallas import tpu as pltpu
from jax.sharding import PartitionSpec as P

HEADS = 32
HEAD = 64
STATE = 128
TOK = 256
LEVELS = 5
HALF = HEADS * HEAD // 2
PACK = STATE + 16
LOG2E = 1.4426950408889634
F32 = jnp.float32
BF16 = jnp.bfloat16
SMEM = pl.BlockSpec(memory_space=pltpu.SMEM)
VMEM = pl.BlockSpec(memory_space=pltpu.VMEM)


def split3(value):
    high = value.astype(BF16)
    rest = value - high.astype(F32)
    middle = rest.astype(BF16)
    low = (rest - middle.astype(F32)).astype(BF16)
    return high, middle, low


def exact_dot(zero_one, value, dims):
    return sum(
        lax.dot_general(zero_one, part, (dims, ((), ())), preferred_element_type=F32) for part in split3(value)
    )


def pad_heads(value):
    return jnp.concatenate([value, jnp.zeros((128 - HEADS, value.shape[1]), F32)], axis=0)


def spread(table, first):
    lane = lax.broadcasted_iota(jnp.int32, table.shape, 1)
    return jnp.take_along_axis(table, jnp.where(lane < HEAD, first, first + 1), axis=1)


def triangle(compare):
    rows = lax.broadcasted_iota(jnp.int32, (TOK, TOK), 0)
    columns = lax.broadcasted_iota(jnp.int32, (TOK, TOK), 1)
    return compare(rows, columns).astype(F32).astype(BF16)


def total_rows(sums):
    row = lax.broadcasted_iota(jnp.int32, sums.shape, 0)
    high, middle, low = (part.astype(F32) for part in split3(sums))
    rows = jnp.where(row == 0, high, jnp.where(row == 1, middle, jnp.where(row == 2, low, 0.0)))
    return rows.astype(BF16)


def read_total(rows):
    return jnp.sum(rows.astype(F32), axis=0, keepdims=True)


def ends_kernel(flags, decay_ref, key_ref, x_ref, packet_ref):
    core = flags[0]
    decay = pad_heads(decay_ref[...])
    after = exact_dot(triangle(lambda r, c: c > r), decay, ((1,), (1,)))
    sums = exact_dot(jnp.ones((16, TOK), BF16), decay, ((1,), (1,)))
    factor = jnp.exp(after)
    keys = key_ref[...]
    for which in range(2):
        half = 1 - core if which == 0 else core
        for chunk in range(HALF // 256):
            pieces = []
            for pair in range(2):
                first = half * (HEADS // 2) + chunk * 4 + pair * 2
                offset = pl.multiple_of(half * HALF + chunk * 256 + pair * 128, 128)
                x = x_ref[:, pl.ds(offset, 128)].astype(F32)
                pieces.append((x * spread(factor, first)).astype(BF16))
                lanes = pl.ds(chunk * 256 + pair * 128, 128)
                packet_ref[which, STATE:PACK, lanes] = total_rows(spread(sums, first))
            decayed = jnp.concatenate(pieces, axis=1)
            state = lax.dot_general(keys, decayed, (((0,), (0,)), ((), ())), preferred_element_type=F32)
            packet_ref[which, 0:STATE, pl.ds(chunk * 256, 256)] = state.astype(BF16)


def make_ends(flags, decay, keys, x):
    return pl.pallas_call(
        ends_kernel,
        out_shape=jax.ShapeDtypeStruct((2, PACK, HALF), BF16),
        in_specs=[SMEM, VMEM, VMEM, VMEM],
        out_specs=VMEM,
        cost_estimate=pl.CostEstimate(flops=2 * TOK * STATE * 2 * HALF, bytes_accessed=2 << 20, transcendentals=32768),
        name="ends",
    )(flags, decay, keys, x)


def merge_kernel(bit, flags, *refs):
    if bit == 0:
        own_ref, got_ref, state_ref, sum_ref, packet_ref = refs
        own = own_ref[0:STATE].astype(F32)
        own_sum = read_total(own_ref[STATE:PACK])
    else:
        own_ref, own_sum_ref, got_ref, state_ref, sum_ref, packet_ref = refs
        own = own_ref[...]
        own_sum = own_sum_ref[0:1]
    right = flags[1 + bit] == 1
    got = got_ref[0:STATE].astype(F32)
    got_sum = read_total(got_ref[STATE:PACK])
    decay = jnp.exp(jnp.where(right, own_sum, got_sum))
    state = jnp.where(right, got, own) * decay + jnp.where(right, own, got)
    sums = own_sum + got_sum
    state_ref[...] = state
    sum_ref[...] = jnp.broadcast_to(sums, (8, HALF))
    packet_ref[0:STATE] = state.astype(BF16)
    packet_ref[STATE:PACK] = total_rows(jnp.broadcast_to(sums, (16, HALF)))


def merge(bit, flags, *arrays):
    return pl.pallas_call(
        functools.partial(merge_kernel, bit),
        out_shape=[
            jax.ShapeDtypeStruct((STATE, HALF), F32),
            jax.ShapeDtypeStruct((8, HALF), F32),
            jax.ShapeDtypeStruct((PACK, HALF), BF16),
        ],
        in_specs=[SMEM] + [VMEM] * len(arrays),
        out_specs=[VMEM] * 3,
        cost_estimate=pl.CostEstimate(flops=1 << 19, bytes_accessed=1 << 20, transcendentals=4096),
        name="merge",
    )(flags, *arrays)


def local_kernel(flags, decay_ref, mix_ref, key_ref, query_ref, x_ref, total_ref, weight_ref, scores, column, row):
    decay = decay_ref[...]
    causal = triangle(lambda r, c: r >= c)
    cum_column = exact_dot(causal, pad_heads(decay), ((1,), (1,)))
    cum_row = cum_column.T[0:HEADS]
    row[...] = cum_row * LOG2E
    column[...] = (cum_column + jnp.log(pad_mix(mix_ref[0])).T) * LOG2E
    gate = jnp.exp(cum_row)
    weights = [
        mix_ref[level + 1] * gate * flags[1 + level].astype(F32) for level in range(LEVELS)
    ]
    weights.append(jnp.zeros((256 - HEADS * LEVELS, TOK), F32))
    weight_ref[...] = jnp.concatenate(weights, axis=0).T
    raw = lax.dot_general(query_ref[...], key_ref[...], (((1,), (1,)), ((), ())), preferred_element_type=F32)
    scores[...] = raw * causal.astype(F32)

    def pair_step(pair, _):
        offset = pl.multiple_of(pair * 128, 128)
        x = x_ref[:, pl.ds(offset, 128)]
        lane = lax.broadcasted_iota(jnp.int32, (TOK, 128), 1)
        result = jnp.zeros((TOK, 128), F32)
        for side in range(2):
            head = pair * 2 + side
            index = jnp.full((TOK, 128), head, jnp.int32)
            col = jnp.take_along_axis(column[...], index, axis=1)
            gap = jnp.concatenate([col, col], axis=1) - row[pl.ds(head, 1)]
            mixing = (scores[...] * jnp.exp2(jnp.minimum(gap, 1.0))).astype(BF16)
            chosen = jnp.where((lane < HEAD) == (side == 0), x, jnp.zeros_like(x))
            result = result + lax.dot_general(
                mixing, chosen, (((1,), (0,)), ((), ())), preferred_element_type=F32
            )
        total_ref[:, pl.ds(offset, 128)] = result
        return 0

    lax.fori_loop(0, HEADS // 2, pair_step, 0)


def pad_mix(value):
    return jnp.concatenate([value, jnp.ones((128 - HEADS, value.shape[1]), F32)], axis=0)


def make_local(flags, decay, mix, keys, queries, x):
    return pl.pallas_call(
        local_kernel,
        out_shape=[
            jax.ShapeDtypeStruct((TOK, 2 * HALF), F32),
            jax.ShapeDtypeStruct((TOK, 256), F32),
        ],
        in_specs=[SMEM] + [VMEM] * 5,
        out_specs=[VMEM] * 2,
        scratch_shapes=[pltpu.VMEM((TOK, TOK), F32), pltpu.VMEM((TOK, 128), F32), pltpu.VMEM((HEADS, TOK), F32)],
        cost_estimate=pl.CostEstimate(
            flops=4 * TOK * TOK * 2 * HALF, bytes_accessed=4 << 20, transcendentals=HEADS * TOK * TOK
        ),
        name="local",
    )(flags, decay, mix, keys, queries, x)


def levels_kernel(count, flags, total_ref, weight_ref, query_ref, *refs):
    packets, (out_ref, gap_ref) = refs[: 2 * count], refs[2 * count :]
    core = flags[0]
    queries = query_ref[...]
    for which in range(2):
        half = core if which == 0 else 1 - core
        gap = jnp.zeros((1, HALF), F32)
        for chunk in range(HALF // 256):
            lanes = pl.ds(chunk * 256, 256)
            columns = pl.ds(pl.multiple_of(half * HALF + chunk * 256, 256), 256)
            running = total_ref[:, columns]
            gap = jnp.zeros((1, 256), F32)
            for level in range(count):
                packet = packets[2 * level + which]
                product = jnp.dot(queries, packet[0:STATE, lanes], preferred_element_type=F32)
                first = level * HEADS + half * (HEADS // 2) + chunk * 4
                table = weight_ref[:, 0:128] if level < 4 else weight_ref[:, 128:256]
                if level >= 4:
                    first = first - 128
                weight = jnp.concatenate([spread(table, first), spread(table, first + 2)], axis=1)
                running = running + product * (weight * jnp.exp(gap))
                gap = gap + read_total(packet[STATE:PACK, lanes]) * flags[1 + level].astype(F32)
            out_ref[:, columns] = running
            gap_ref[:, pl.ds(which * HALF + chunk * 256, 256)] = jnp.broadcast_to(gap, (8, 256))


def add_levels(flags, total, weights, queries, *packets):
    count = len(packets) // 2
    return pl.pallas_call(
        functools.partial(levels_kernel, count),
        out_shape=[
            jax.ShapeDtypeStruct((TOK, 2 * HALF), F32),
            jax.ShapeDtypeStruct((8, 2 * HALF), F32),
        ],
        in_specs=[SMEM] + [VMEM] * (3 + 2 * count),
        out_specs=[VMEM] * 2,
        input_output_aliases={1: 0},
        cost_estimate=pl.CostEstimate(
            flops=2 * count * TOK * STATE * 2 * HALF, bytes_accessed=6 << 20, transcendentals=0
        ),
        name="levels",
    )(flags, total, weights, queries, *packets)


def last_kernel(flags, total_ref, gap_ref, weight_ref, query_ref, mine_ref, other_ref, out_ref):
    core = flags[0]
    queries = query_ref[...]
    table = weight_ref[:, 128:256]
    for which, packet in enumerate((mine_ref, other_ref)):
        half = core if which == 0 else 1 - core
        for chunk in range(HALF // 256):
            lanes = pl.ds(chunk * 256, 256)
            columns = pl.ds(pl.multiple_of(half * HALF + chunk * 256, 256), 256)
            product = jnp.dot(queries, packet[0:STATE, lanes], preferred_element_type=F32)
            first = half * (HEADS // 2) + chunk * 4
            weight = jnp.concatenate([spread(table, first), spread(table, first + 2)], axis=1)
            gap = gap_ref[0:1, pl.ds(which * HALF + chunk * 256, 256)]
            out_ref[:, columns] = (total_ref[:, columns] + product * (weight * jnp.exp(gap))).astype(BF16)


def add_last(flags, total, gap, weights, queries, mine, other):
    return pl.pallas_call(
        last_kernel,
        out_shape=jax.ShapeDtypeStruct((TOK, 2 * HALF), BF16),
        in_specs=[SMEM] + [VMEM] * 6,
        out_specs=VMEM,
        cost_estimate=pl.CostEstimate(
            flops=2 * TOK * STATE * 2 * HALF, bytes_accessed=4 << 20, transcendentals=0
        ),
        name="last",
    )(flags, total, gap, weights, queries, mine, other)


def body(inputs, write_keys, read_queries, decay_log, level_mix):
    devices = lax.axis_size("ctx")
    index = lax.axis_index("ctx")
    shifts = jnp.array([0, 0, 1, 2, 3, 4, 0, 0], jnp.int32)
    flags = (index >> shifts) & 1

    def swap(array, mask):
        return lax.ppermute(array, "ctx", [(i, i ^ mask) for i in range(devices)])

    packets = make_ends(flags, decay_log, write_keys, inputs)
    mine = [swap(packets[0], 1)]
    other = [swap(packets[1], 1)]
    total, weights = make_local(flags, decay_log, level_mix, write_keys, read_queries, inputs)
    state, sums, packet = merge(0, flags, packets[1], mine[0])
    for level in range(1, LEVELS):
        got = swap(packet, {1: 2, 2: 6, 3: 8, 4: 24}[level])
        mine.append(got)
        other.append(swap(got, 1))
        if level < LEVELS - 1:
            state, sums, packet = merge(level, flags, state, sums, got)
    order = [p for pair in zip(mine[:4], other[:4]) for p in pair]
    total, gap = add_levels(flags, total, weights, read_queries, *order)
    return add_last(flags, total, gap, weights, read_queries, mine[4], other[4])


def solution(mesh):
    placed = (
        P(("seq", "ctx"), None),
        P(("seq", "ctx"), None),
        P(("seq", "ctx"), None),
        P(None, ("seq", "ctx")),
        P(None, None, ("seq", "ctx")),
    )
    return jax.shard_map(
        body, mesh=mesh, in_specs=placed, out_specs=P(("seq", "ctx"), None), check_vma=False
    )
```

```python
import functools

import jax
import jax.numpy as jnp
from jax import lax
from jax.experimental import pallas as pl
from jax.experimental.pallas import tpu as pltpu
from jax.sharding import PartitionSpec as P

HEADS = 32
HEAD = 64
STATE = 128
TOK = 256
LEVELS = 5
HALF = HEADS * HEAD // 2
PAIRS = HEADS // 4
BODY = PAIRS * STATE
PACK = BODY + 16
LOG2E = 1.4426950408889634
F32 = jnp.float32
BF16 = jnp.bfloat16
VMEM = pl.BlockSpec(memory_space=pltpu.VMEM)
ANY = pl.BlockSpec(memory_space=pl.ANY)
KEPT = pltpu.MemorySpace.VMEM
PACKET = pltpu.VMEM((PACK, 128), BF16)
SUMS = pltpu.VMEM((8, 128), F32)


def split3(value):
    high = value.astype(BF16)
    rest = value - high.astype(F32)
    middle = rest.astype(BF16)
    low = (rest - middle.astype(F32)).astype(BF16)
    return high, middle, low


def exact_dot(zero_one, value, dims):
    return sum(
        lax.dot_general(zero_one, part, (dims, ((), ())), preferred_element_type=F32) for part in split3(value)
    )


def pad_heads(value):
    return jnp.concatenate([value, jnp.zeros((128 - HEADS, value.shape[1]), F32)], axis=0)


def spread(table, first):
    lane = lax.broadcasted_iota(jnp.int32, table.shape, 1)
    return jnp.take_along_axis(table, jnp.where(lane < HEAD, first, first + 1), axis=1)


def triangle(compare):
    rows = lax.broadcasted_iota(jnp.int32, (TOK, TOK), 0)
    columns = lax.broadcasted_iota(jnp.int32, (TOK, TOK), 1)
    return compare(rows, columns).astype(F32).astype(BF16)


def total_rows(sums):
    row = lax.broadcasted_iota(jnp.int32, sums.shape, 0)
    high, middle, low = (part.astype(F32) for part in split3(sums))
    rows = jnp.where(row == 0, high, jnp.where(row == 1, middle, jnp.where(row == 2, low, 0.0)))
    return rows.astype(BF16)


def read_total(rows):
    return jnp.sum(rows.astype(F32), axis=0, keepdims=True)


def position():
    index = lax.axis_index("ctx")
    return [(index >> bit) & 1 for bit in range(LEVELS)]


def call(kernel, outs, arrays, name, flops, exps=0, kept=(), far=(), out_specs=None, scratch=(), aliases=None):
    arrays = list(arrays)
    for place in kept:
        arrays[place] = pltpu.with_memory_space_constraint(arrays[place], KEPT)
    for place in far:
        arrays[place] = pltpu.with_memory_space_constraint(arrays[place], pltpu.MemorySpace.HBM)
    return pl.pallas_call(
        kernel,
        out_shape=outs,
        in_specs=[ANY if place in far else VMEM for place in range(len(arrays))],
        out_specs=out_specs or [VMEM] * len(outs),
        scratch_shapes=list(scratch),
        input_output_aliases=aliases or {},
        compiler_params=pltpu.CompilerParams(vmem_limit_bytes=20 << 20),
        cost_estimate=pl.CostEstimate(flops=flops, bytes_accessed=1 << 20, transcendentals=exps),
        name=name,
    )(*arrays)


def ends_kernel(decay_hbm, key_hbm, x_hbm, sent_ref, kept_ref, decay_ref, key_ref, x_ref, small, big):
    core = position()[0]
    copies = [
        pltpu.make_async_copy(decay_hbm, decay_ref, small.at[0]), pltpu.make_async_copy(key_hbm, key_ref, small.at[1])
    ]
    halves = (1 - core, core)
    for place, half in enumerate(halves):
        for chunk in range(2):
            columns = pl.ds(pl.multiple_of(half * HALF + chunk * 512, 512), 512)
            copies.append(
                pltpu.make_async_copy(x_hbm.at[:, columns], x_ref.at[:, columns], big.at[2 * place + chunk])
            )
    for copy in copies:
        copy.start()
    copies[0].wait()
    decay = pad_heads(decay_ref[...])
    after = exact_dot(triangle(lambda r, c: c > r), decay, ((1,), (1,)))
    sums = exact_dot(jnp.ones((16, TOK), BF16), decay, ((1,), (1,)))
    factor = jnp.exp(after)
    lane = lax.broadcasted_iota(jnp.int32, sums.shape, 1)
    copies[1].wait()
    keys = key_ref[...]
    for place, (half, packet_ref) in enumerate(zip(halves, (sent_ref, kept_ref))):
        packet_ref[BODY:PACK] = total_rows(jnp.take_along_axis(sums, (lane + half * (HEADS // 2)) & 127, axis=1))
        for duo in range(PAIRS // 2):
            if duo % 2 == 0:
                copies[2 + 2 * place + duo // 2].wait()
            pieces = []
            for pair in (2 * duo, 2 * duo + 1):
                x = x_ref[:, pl.ds(pl.multiple_of(half * HALF + pair * 128, 128), 128)].astype(F32)
                pieces.append((x * spread(factor, half * (HEADS // 2) + pair * 2)).astype(BF16))
            decayed = jnp.concatenate(pieces, axis=1)
            state = lax.dot_general(keys, decayed, (((0,), (0,)), ((), ())), preferred_element_type=F32)
            packet_ref[duo * 256 : duo * 256 + 128] = state[:, 0:128].astype(BF16)
            packet_ref[duo * 256 + 128 : duo * 256 + 256] = state[:, 128:256].astype(BF16)


def merge_kernel(bit, *refs):
    if bit == 0:
        own_ref, got_ref, state_ref, sum_ref, packet_ref = refs
        own_sum = read_total(own_ref[BODY:PACK])
    else:
        own_ref, own_sum_ref, got_ref, state_ref, sum_ref, packet_ref = refs
        own_sum = own_sum_ref[0:1]
    right = position()[bit] == 1
    got_sum = read_total(got_ref[BODY:PACK])
    decay = jnp.broadcast_to(jnp.exp(jnp.where(right, own_sum, got_sum)), (8, 128))
    sums = own_sum + got_sum
    sum_ref[...] = jnp.broadcast_to(sums, (8, 128))
    packet_ref[BODY:PACK] = total_rows(jnp.broadcast_to(sums, (16, 128)))
    for pair in range(PAIRS):
        rows = pl.ds(pair * STATE, STATE)
        own = own_ref[rows].astype(F32)
        got = got_ref[rows].astype(F32)
        factor = spread(decay, 2 * pair)[0:1]
        state = jnp.where(right, got, own) * factor + jnp.where(right, own, got)
        state_ref[rows] = state
        packet_ref[rows] = state.astype(BF16)


def merge(bit, *arrays):
    outs = [pltpu.VMEM((BODY, 128), F32), SUMS, PACKET]
    return call(functools.partial(merge_kernel, bit), outs, arrays, "merge", 1 << 19, 4096, range(len(arrays)))


def local_kernel(other, decay_ref, mix_ref, key_ref, query_ref, x_ref, *refs):
    if other:
        total_ref, scores, column, row = refs
    else:
        total_ref, weight_ref, scores, column, row = refs
    bits = position()
    half = 1 - bits[0] if other else bits[0]
    decay = decay_ref[...]
    causal = triangle(lambda r, c: r >= c)
    cum_column = exact_dot(causal, pad_heads(decay), ((1,), (1,)))
    cum_row = cum_column.T[0:HEADS]
    row[...] = cum_row * LOG2E
    mix = jnp.concatenate([mix_ref[0], jnp.ones((128 - HEADS, TOK), F32)], axis=0)
    column[...] = (cum_column + jnp.log(mix).T) * LOG2E
    if not other:
        gate = jnp.exp(cum_row)
        weights = [mix_ref[level + 1] * gate * bits[level].astype(F32) for level in range(LEVELS)]
        weights.append(jnp.zeros((256 - HEADS * LEVELS, TOK), F32))
        weight_ref[...] = jnp.concatenate(weights, axis=0).T
    raw = lax.dot_general(query_ref[...], key_ref[...], (((1,), (1,)), ((), ())), preferred_element_type=F32)
    scores[...] = raw * causal.astype(F32)

    def pair_step(pair, _):
        offset = pl.multiple_of(half * HALF + pair * 128, 128)
        x = x_ref[:, pl.ds(offset, 128)]
        lane = lax.broadcasted_iota(jnp.int32, (TOK, 128), 1)
        result = jnp.zeros((TOK, 128), F32)
        for side in range(2):
            head = half * (HEADS // 2) + pair * 2 + side
            index = jnp.full((TOK, 128), head, jnp.int32)
            col = jnp.take_along_axis(column[...], index, axis=1)
            gap = jnp.concatenate([col, col], axis=1) - row[pl.ds(head, 1)]
            mixing = (scores[...] * jnp.exp2(jnp.minimum(gap, 1.0))).astype(BF16)
            chosen = jnp.where((lane < HEAD) == (side == 0), x, jnp.zeros_like(x))
            result = result + lax.dot_general(
                mixing, chosen, (((1,), (0,)), ((), ())), preferred_element_type=F32
            )
        total_ref[:, pl.ds(pl.multiple_of(pair * 128, 128), 128)] = result
        return 0

    lax.fori_loop(0, PAIRS, pair_step, 0)


def make_local(other, *arrays):
    outs = [pltpu.VMEM((TOK, HALF), F32)]
    if not other:
        outs.append(pltpu.VMEM((TOK, 256), F32))
    scratch = [pltpu.VMEM((TOK, TOK), F32), pltpu.VMEM((TOK, 128), F32), pltpu.VMEM((HEADS, TOK), F32)]
    return call(
        functools.partial(local_kernel, other), outs, arrays, "local",
        4 * TOK * TOK * HALF, HEADS // 2 * TOK * TOK, kept=(0, 2, 4), scratch=scratch,
    )


def duo_columns(packet_ref, duo):
    rows = duo * 256
    return jnp.concatenate([packet_ref[rows : rows + 128], packet_ref[rows + 128 : rows + 256]], axis=1)


def duo_spread(table, first):
    return jnp.concatenate([spread(table, first), spread(table, first + 2)], axis=1)


def level_term(level, half, duo, queries, packet_ref, weight_ref, gap):
    product = jnp.dot(queries, duo_columns(packet_ref, duo), preferred_element_type=F32)
    first = (level * HEADS) % 128 + half * (HEADS // 2) + duo * 4
    table = weight_ref[:, 0:128] if level < 4 else weight_ref[:, 128:256]
    return product * (duo_spread(table, first) * duo_spread(gap, duo * 4)[0:1])


def levels_kernel(other, wanted, total_ref, gap_ref, weight_ref, query_ref, *refs):
    packets, (out_ref, gap_out_ref) = refs[: len(wanted)], refs[len(wanted) :]
    bits = position()
    half = 1 - bits[0] if other else bits[0]
    queries = query_ref[...]
    gap, gaps = gap_ref[...], []
    for level, packet in zip(wanted, packets):
        gaps.append(jnp.exp(gap))
        gap = gap + read_total(packet[BODY:PACK]) * bits[level].astype(F32)
    gap_out_ref[...] = gap
    for duo in range(PAIRS // 2):
        lanes = pl.ds(duo * 256, 256)
        running = total_ref[:, lanes]
        for level, packet, before in zip(wanted, packets, gaps):
            running = running + level_term(level, half, duo, queries, packet, weight_ref, before)
        out_ref[:, lanes] = running


def add_levels(other, wanted, total, gap, weights, queries, *packets):
    outs = [pltpu.VMEM((TOK, HALF), F32), SUMS]
    return call(
        functools.partial(levels_kernel, other, wanted), outs, [total, gap, weights, queries, *packets], "levels",
        2 * len(wanted) * TOK * STATE * HALF, kept=(0, 1, 2, *range(4, 4 + len(wanted))), aliases={0: 0, 1: 1},
    )


def first_last_kernel(total_ref, gap_ref, weight_ref, query_ref, packet_ref, out_ref):
    half = position()[0]
    queries = query_ref[...]
    gap = jnp.exp(gap_ref[...])
    for duo in range(PAIRS // 2):
        lanes = pl.ds(duo * 256, 256)
        term = level_term(LEVELS - 1, half, duo, queries, packet_ref, weight_ref, gap)
        out_ref[:, lanes] = (total_ref[:, lanes] + term).astype(BF16)


def second_last_kernel(done_ref, total_ref, gap_ref, weight_ref, query_ref, packet_ref, out_ref, buffer, done_sem, sems):
    core = position()[0]
    half = 1 - core
    mine = pltpu.make_async_copy(
        done_ref, out_ref.at[:, pl.ds(pl.multiple_of(core * HALF, HALF), HALF)], done_sem
    )
    mine.start()
    queries = query_ref[...]
    gap = jnp.exp(gap_ref[...])
    copies = []
    for duo in range(PAIRS // 2):
        lanes = pl.ds(duo * 256, 256)
        term = level_term(LEVELS - 1, half, duo, queries, packet_ref, weight_ref, gap)
        buffer[duo] = (total_ref[:, lanes] + term).astype(BF16)
        columns = pl.ds(pl.multiple_of(half * HALF + duo * 256, 256), 256)
        copies.append(pltpu.make_async_copy(buffer.at[duo], out_ref.at[:, columns], sems.at[duo]))
        copies[-1].start()
    mine.wait()
    for copy in copies:
        copy.wait()


def body(inputs, write_keys, read_queries, decay_log, level_mix):
    devices = lax.axis_size("ctx")

    def swap(array, mask):
        return lax.ppermute(array, "ctx", [(i, i ^ mask) for i in range(devices)])

    def after(*arrays):
        return lax.optimization_barrier(arrays)

    masks = (1, 2, 6, 8, 24)
    sent, kept, decay, keys, x = call(
        ends_kernel,
        [PACKET, PACKET, pltpu.VMEM((HEADS, TOK), F32), pltpu.VMEM((TOK, STATE), BF16), pltpu.VMEM((TOK, 2 * HALF), BF16)],
        [decay_log, write_keys, inputs], "ends", 4 * TOK * STATE * HALF, 32768, far=(0, 1, 2),
        scratch=[pltpu.SemaphoreType.DMA((2,)), pltpu.SemaphoreType.DMA((4,))],
    )
    mine = [swap(sent, 1)]
    state, sums, packet = merge(0, kept, mine[0])
    got = swap(packet, masks[1])
    other = [swap(kept, 1)]
    total, weights = make_local(False, decay, level_mix, keys, read_queries, x)
    zero = jnp.zeros((8, 128), F32)
    got, total, weights = after(got, total, weights)
    mine.append(got)
    state, sums, packet = merge(1, state, sums, got)
    got = swap(packet, masks[2])
    other.append(swap(mine[1], 1))
    other_total, = make_local(True, decay, level_mix, keys, read_queries, x)
    got, other_total = after(got, other_total)
    mine.append(got)
    state, sums, packet = merge(2, state, sums, got)
    got = swap(packet, masks[3])
    other.append(swap(mine[2], 1))
    total, gap = add_levels(False, (0, 1, 2), total, zero, weights, read_queries, *mine)
    got, total, gap = after(got, total, gap)
    mine.append(got)
    state, sums, packet = merge(3, state, sums, got)
    got = swap(packet, masks[4])
    other.append(swap(mine[3], 1))
    total, gap = add_levels(False, (3,), total, gap, weights, read_queries, mine[3])
    other_total, other_gap = add_levels(True, (0, 1, 2, 3), other_total, zero, weights, read_queries, *other)
    got, total, gap, other_total, other_gap = after(got, total, gap, other_total, other_gap)
    got_other = swap(got, 1)
    flops = 2 * TOK * STATE * HALF
    done, = call(
        first_last_kernel, [pltpu.VMEM((TOK, HALF), BF16)], [total, gap, weights, read_queries, got], "last", flops,
        kept=(0, 1, 2, 4),
    )
    got_other, done = after(got_other, done)
    out, = call(
        second_last_kernel, [jax.ShapeDtypeStruct((TOK, 2 * HALF), BF16)],
        [done, other_total, other_gap, weights, read_queries, got_other], "last", flops, kept=(0, 1, 2, 3, 5),
        out_specs=[ANY],
        scratch=[
            pltpu.VMEM((PAIRS // 2, TOK, 256), BF16), pltpu.SemaphoreType.DMA, pltpu.SemaphoreType.DMA((PAIRS // 2,))
        ],
    )
    return out


def solution(mesh):
    placed = (
        P(("seq", "ctx"), None),
        P(("seq", "ctx"), None),
        P(("seq", "ctx"), None),
        P(None, ("seq", "ctx")),
        P(None, None, ("seq", "ctx")),
    )
    return jax.shard_map(
        body, mesh=mesh, in_specs=placed, out_specs=P(("seq", "ctx"), None), check_vma=False
    )
```

```python
import functools

import jax
import jax.numpy as jnp
from jax import lax
from jax.experimental import pallas as pl
from jax.experimental.pallas import tpu as pltpu
from jax.sharding import PartitionSpec as P

HEADS = 32
HEAD = 64
STATE = 128
TOK = 256
LEVELS = 5
SHARE = HEADS // 2
CHUNKS = 2
PAIRS = SHARE // 2 // CHUNKS
WIDTH = PAIRS * 128
BODY = PAIRS * STATE
PACK = BODY + 16
LOG2E = 1.4426950408889634
F32 = jnp.float32
BF16 = jnp.bfloat16
VMEM = pl.BlockSpec(memory_space=pltpu.VMEM)
ANY = pl.BlockSpec(memory_space=pl.ANY)
KEPT = pltpu.MemorySpace.VMEM
PACKET = pltpu.VMEM((PACK, 128), BF16)
SUMS = pltpu.VMEM((8, 128), F32)
TABLE = pltpu.VMEM((TOK, 128), F32)
PART = pltpu.VMEM((TOK, WIDTH), F32)
X_PART = pltpu.VMEM((2, TOK, WIDTH), BF16)


def split3(value):
    high = value.astype(BF16)
    rest = value - high.astype(F32)
    middle = rest.astype(BF16)
    low = (rest - middle.astype(F32)).astype(BF16)
    return high, middle, low


def exact_dot(zero_one, value, dims):
    return sum(
        lax.dot_general(zero_one, part, (dims, ((), ())), preferred_element_type=F32) for part in split3(value)
    )


def pad_heads(value):
    return jnp.concatenate([value, jnp.zeros((128 - HEADS, value.shape[1]), F32)], axis=0)


def spread(table, first):
    lane = lax.broadcasted_iota(jnp.int32, table.shape, 1)
    return jnp.take_along_axis(table, jnp.where(lane < HEAD, first, first + 1), axis=1)


def triangle(compare):
    rows = lax.broadcasted_iota(jnp.int32, (TOK, TOK), 0)
    columns = lax.broadcasted_iota(jnp.int32, (TOK, TOK), 1)
    return compare(rows, columns).astype(F32).astype(BF16)


def total_rows(sums):
    row = lax.broadcasted_iota(jnp.int32, sums.shape, 0)
    high, middle, low = (part.astype(F32) for part in split3(sums))
    rows = jnp.where(row == 0, high, jnp.where(row == 1, middle, jnp.where(row == 2, low, 0.0)))
    return rows.astype(BF16)


def read_total(rows):
    return jnp.sum(rows.astype(F32), axis=0, keepdims=True)


def position():
    index = lax.axis_index("ctx")
    return [(index >> bit) & 1 for bit in range(LEVELS)]


def call(kernel, outs, arrays, name, flops, exps=0, kept=(), far=(), out_specs=None, scratch=(), aliases=None):
    arrays = list(arrays)
    for place in kept:
        arrays[place] = pltpu.with_memory_space_constraint(arrays[place], KEPT)
    for place in far:
        arrays[place] = pltpu.with_memory_space_constraint(arrays[place], pltpu.MemorySpace.HBM)
    return pl.pallas_call(
        kernel,
        out_shape=outs,
        in_specs=[ANY if place in far else VMEM for place in range(len(arrays))],
        out_specs=out_specs or [VMEM] * len(outs),
        scratch_shapes=list(scratch),
        input_output_aliases=aliases or {},
        compiler_params=pltpu.CompilerParams(vmem_limit_bytes=20 << 20),
        cost_estimate=pl.CostEstimate(flops=flops, bytes_accessed=1 << 20, transcendentals=exps),
        name=name,
    )(*arrays)


def ends_kernel(chunk, *refs):
    core = position()[0]
    if chunk == 0:
        decay_hbm, key_hbm, x_hbm, sent_ref, kept_ref, x_ref, decay_ref, key_ref, factor_ref, sum_ref, small, big = refs
    else:
        x_hbm, key_ref, factor_ref, sum_ref, sent_ref, kept_ref, x_ref, big = refs
    halves = (1 - core, core)
    copies = []
    if chunk == 0:
        copies.append(pltpu.make_async_copy(decay_hbm, decay_ref, small.at[0]))
        copies.append(pltpu.make_async_copy(key_hbm, key_ref, small.at[1]))
    for place, half in enumerate(halves):
        columns = pl.ds(pl.multiple_of(half * (CHUNKS * WIDTH) + chunk * WIDTH, WIDTH), WIDTH)
        copies.append(pltpu.make_async_copy(x_hbm.at[:, columns], x_ref.at[place], big.at[place]))
    for copy in copies:
        copy.start()
    if chunk == 0:
        copies[0].wait()
        decay = pad_heads(decay_ref[...])
        after = exact_dot(triangle(lambda r, c: c > r), decay, ((1,), (1,)))
        sums = exact_dot(jnp.ones((16, TOK), BF16), decay, ((1,), (1,)))
        factor = jnp.exp(after)
        factor_ref[...] = factor
        sum_ref[...] = sums
        copies[1].wait()
    else:
        factor = factor_ref[...]
        sums = sum_ref[...]
    lane = lax.broadcasted_iota(jnp.int32, sums.shape, 1)
    keys = key_ref[...]
    for place, (half, packet_ref) in enumerate(zip(halves, (sent_ref, kept_ref))):
        packet_ref[BODY:PACK] = total_rows(jnp.take_along_axis(sums, (lane + half * SHARE) & 127, axis=1))
        copies[place - 2].wait()
        for duo in range(PAIRS // 2):
            pieces = []
            for pair in (2 * duo, 2 * duo + 1):
                x = x_ref[place, :, pair * 128 : pair * 128 + 128].astype(F32)
                pieces.append((x * spread(factor, half * SHARE + (chunk * PAIRS + pair) * 2)).astype(BF16))
            decayed = jnp.concatenate(pieces, axis=1)
            state = lax.dot_general(keys, decayed, (((0,), (0,)), ((), ())), preferred_element_type=F32)
            packet_ref[duo * 256 : duo * 256 + 128] = state[:, 0:128].astype(BF16)
            packet_ref[duo * 256 + 128 : duo * 256 + 256] = state[:, 128:256].astype(BF16)


def merge_kernel(bit, chunk, *refs):
    state_ref = sum_ref = None
    if bit == 0:
        own_ref, got_ref, packet_ref, state_ref, sum_ref = refs
        own_sum = read_total(own_ref[BODY:PACK])
    else:
        own_ref, own_sum_ref, got_ref, packet_ref = refs[:4]
        own_sum = own_sum_ref[0:1]
        if bit < LEVELS - 2:
            state_ref, sum_ref = refs[4:]
    right = position()[bit] == 1
    got_sum = read_total(got_ref[BODY:PACK])
    decay = jnp.broadcast_to(jnp.exp(jnp.where(right, own_sum, got_sum)), (8, 128))
    sums = own_sum + got_sum
    if sum_ref is not None:
        sum_ref[...] = jnp.broadcast_to(sums, (8, 128))
    packet_ref[BODY:PACK] = total_rows(jnp.broadcast_to(sums, (16, 128)))
    for pair in range(PAIRS):
        rows = pl.ds(pair * STATE, STATE)
        own = own_ref[rows].astype(F32)
        got = got_ref[rows].astype(F32)
        factor = spread(decay, 2 * (chunk * PAIRS + pair))[0:1]
        state = jnp.where(right, got, own) * factor + jnp.where(right, own, got)
        if state_ref is not None:
            state_ref[rows] = state
        packet_ref[rows] = state.astype(BF16)


def merge(bit, chunk, *arrays):
    outs = [PACKET] + ([pltpu.VMEM((BODY, 128), F32), SUMS] if bit < LEVELS - 2 else [])
    return call(
        functools.partial(merge_kernel, bit, chunk), outs, arrays, "merge", 1 << 19, 4096, range(len(arrays))
    )


def tables_kernel(decay_ref, mix_ref, key_ref, query_ref, scores_ref, column_ref, row_ref, own_ref, sent_ref):
    bits = position()
    core = bits[0]
    decay = decay_ref[...]
    causal = triangle(lambda r, c: r >= c)
    cum_column = exact_dot(causal, pad_heads(decay), ((1,), (1,)))
    cum_row = cum_column.T[0:HEADS]
    row_ref[...] = cum_row * LOG2E
    mix = jnp.concatenate([mix_ref[0], jnp.ones((128 - HEADS, TOK), F32)], axis=0)
    column_ref[...] = (cum_column + jnp.log(mix).T) * LOG2E
    gate = jnp.exp(cum_row)
    weights = [mix_ref[level + 1] * gate * bits[level].astype(F32) for level in range(LEVELS)]
    unused = [jnp.zeros((128 - SHARE * LEVELS, TOK), F32)]
    low = jnp.concatenate([weight[:SHARE] for weight in weights] + unused, axis=0).T
    high = jnp.concatenate([weight[SHARE:] for weight in weights] + unused, axis=0).T
    own_ref[...] = jnp.where(core == 0, low, high)
    sent_ref[...] = jnp.where(core == 0, high, low)
    raw = lax.dot_general(query_ref[...], key_ref[...], (((1,), (1,)), ((), ())), preferred_element_type=F32)
    scores_ref[...] = raw * causal.astype(F32)


def local_kernel(place, chunk, scores_ref, column_ref, row_ref, x_ref, total_ref):
    core = position()[0]
    half = core if place == 1 else 1 - core
    upper = TOK // 2
    lane = lax.broadcasted_iota(jnp.int32, (TOK, 128), 1)

    def pair_step(pair, _):
        offset = pl.multiple_of(pair * 128, 128)
        x = x_ref[place, :, pl.ds(offset, 128)]
        top = jnp.zeros((upper, 128), F32)
        bottom = jnp.zeros((upper, 128), F32)
        for side in range(2):
            head = half * SHARE + (chunk * PAIRS + pair) * 2 + side
            column = jnp.take_along_axis(column_ref[...], jnp.full((TOK, 128), head, jnp.int32), axis=1)
            row = row_ref[pl.ds(head, 1)]
            chosen = jnp.where((lane < HEAD) == (side == 0), x, jnp.zeros_like(x))
            gap = column[:upper] - row[:, :upper]
            mixing = (scores_ref[:upper, :upper] * jnp.exp2(jnp.minimum(gap, 1.0))).astype(BF16)
            top = top + jnp.dot(mixing, chosen[:upper], preferred_element_type=F32)
            below = column[upper:]
            gap = jnp.concatenate([below, below], axis=1) - row
            mixing = (scores_ref[upper:] * jnp.exp2(jnp.minimum(gap, 1.0))).astype(BF16)
            bottom = bottom + jnp.dot(mixing, chosen, preferred_element_type=F32)
        total_ref[:upper, pl.ds(offset, 128)] = top
        total_ref[upper:, pl.ds(offset, 128)] = bottom
        return 0

    lax.fori_loop(0, PAIRS, pair_step, 0)


def make_local(place, chunk, *arrays):
    return call(
        functools.partial(local_kernel, place, chunk), [PART], arrays, "local", 4 * TOK * TOK * WIDTH,
        2 * PAIRS * TOK * TOK, kept=range(4),
    )[0]


def duo_columns(packet_ref, duo):
    rows = duo * 256
    return jnp.concatenate([packet_ref[rows : rows + 128], packet_ref[rows + 128 : rows + 256]], axis=1)


def duo_spread(table, first):
    return jnp.concatenate([spread(table, first), spread(table, first + 2)], axis=1)


def level_term(level, chunk, duo, queries, packet_ref, weight_ref, gap):
    product = jnp.dot(queries, duo_columns(packet_ref, duo), preferred_element_type=F32)
    pair = chunk * PAIRS + duo * 2
    return product * (duo_spread(weight_ref[...], level * SHARE + pair * 2) * duo_spread(gap, pair * 2)[0:1])


def levels_kernel(wanted, chunk, *refs):
    bits = position()
    weight_refs, query_refs = refs[0:2], refs[2:4]
    if wanted[0] == 0:
        total_ref, kept_ref, *packets = refs[4:-4]
        totals = (total_ref, None)
        gaps = [jnp.zeros((8, 128), F32)] * 2
    else:
        totals, gaps, packets = refs[4:6], [refs[6][...], refs[7][...]], refs[8:-4]
        kept_ref = None
    outs, gap_outs = refs[-4:-2], refs[-2:]
    for side in range(2):
        queries = query_refs[side][...]
        used = [kept_ref if side == 1 and level == 0 else packet for level, packet in zip(wanted, packets)]
        gap, before = gaps[side], []
        for level, packet in zip(wanted, used):
            before.append(jnp.exp(gap))
            bit = 1 - bits[0] if side == 1 and level == 0 else bits[level]
            gap = gap + read_total(packet[BODY:PACK]) * bit.astype(F32)
        gap_outs[side][...] = gap
        for duo in range(PAIRS // 2):
            lanes = slice(duo * 256, duo * 256 + 256)
            running = None if totals[side] is None else totals[side][:, lanes]
            for level, packet, factor in zip(wanted, used, before):
                term = level_term(level, chunk, duo, queries, packet, weight_refs[side], factor)
                running = term if running is None else running + term
            outs[side][:, lanes] = running


def add_levels(wanted, chunk, *arrays):
    return call(
        functools.partial(levels_kernel, wanted, chunk), [PART, PART, SUMS, SUMS], arrays, "levels",
        4 * len(wanted) * TOK * STATE * WIDTH, kept=range(len(arrays)),
    )


def last_kernel(chunk, weight_ref, query_ref, total_ref, gap_ref, packet_ref, out_ref):
    queries = query_ref[...]
    gap = jnp.exp(gap_ref[...])
    for duo in range(PAIRS // 2):
        lanes = slice(duo * 256, duo * 256 + 256)
        term = level_term(LEVELS - 1, chunk, duo, queries, packet_ref, weight_ref, gap)
        out_ref[:, lanes] = (total_ref[:, lanes] + term).astype(BF16)


def add_last(chunk, *arrays):
    return call(
        functools.partial(last_kernel, chunk), [pltpu.VMEM((TOK, WIDTH), BF16)], arrays, "last",
        2 * TOK * STATE * WIDTH, kept=range(5),
    )[0]


def finish_kernel(*refs):
    done, totals, parts = refs[:CHUNKS], refs[CHUNKS : 2 * CHUNKS], refs[2 * CHUNKS : 3 * CHUNKS]
    out_ref, buffer, sems = refs[3 * CHUNKS :]
    core = position()[0]
    copies = []

    def send(source, half, chunk):
        columns = pl.ds(pl.multiple_of(half * (CHUNKS * WIDTH) + chunk * WIDTH, WIDTH), WIDTH)
        copies.append(pltpu.make_async_copy(source, out_ref.at[:, columns], sems.at[len(copies)]))
        copies[-1].start()

    for chunk in range(CHUNKS):
        send(done[chunk], core, chunk)
    for chunk in range(CHUNKS):
        buffer[chunk] = (totals[chunk][...] + parts[chunk][...].astype(F32)).astype(BF16)
        send(buffer.at[chunk], 1 - core, chunk)
    for copy in copies:
        copy.wait()


def body(inputs, write_keys, read_queries, decay_log, level_mix):
    devices = lax.axis_size("ctx")

    def swap(array, mask):
        return lax.ppermute(array, "ctx", [(i, i ^ mask) for i in range(devices)])

    def after(*arrays):
        return lax.optimization_barrier(arrays)

    chunks = range(CHUNKS)
    masks = (1, 2, 6, 8, 24)
    kept, x, got, state, packet = ([None] * CHUNKS for _ in range(5))
    history = [[] for _ in chunks]
    for c in chunks:
        semaphores = pltpu.SemaphoreType.DMA((2,))
        kernel, flops = functools.partial(ends_kernel, c), 4 * TOK * STATE * WIDTH
        if c == 0:
            sent, kept[c], x[c], decay, keys, factor, sums = call(
                kernel,
                [
                    PACKET, PACKET, X_PART, pltpu.VMEM((HEADS, TOK), F32), pltpu.VMEM((TOK, STATE), BF16), TABLE,
                    pltpu.VMEM((16, 128), F32),
                ],
                [decay_log, write_keys, inputs], "ends", flops, 32768, far=(0, 1, 2), scratch=[semaphores, semaphores],
            )
        else:
            sent, kept[c], x[c] = call(
                kernel, [PACKET, PACKET, X_PART], [inputs, keys, factor, sums], "ends", flops, far=(0,),
                kept=(1, 2, 3), scratch=[semaphores],
            )
        got[c] = swap(sent, masks[0])

    def advance(level, c):
        history[c].append(got[c])
        if level == 0:
            packet[c], *state[c] = merge(0, c, kept[c], got[c])
        else:
            packet[c], *state[c] = merge(level, c, *state[c], got[c])
        got[c] = swap(packet[c], masks[level + 1])

    for c in chunks:
        advance(0, c)
    queries, level_mix, _ = after(read_queries, level_mix, packet[-1])
    scores, column, row, weights, sent = call(
        tables_kernel, [pltpu.VMEM((TOK, TOK), F32), TABLE, pltpu.VMEM((HEADS, TOK), F32), TABLE, TABLE],
        [decay, level_mix, keys, queries], "tables", 4 * TOK * TOK * STATE, 16384, kept=(0, 1, 2, 3),
    )
    far_weights, far_queries = swap(sent, 1), swap(queries, 1)
    total, rest = [None] * CHUNKS, [None] * CHUNKS
    for level, place, results in ((1, 1, total), (2, 0, rest)):
        for c in chunks:
            results[c] = make_local(place, c, scores, column, row, x[c])
            got[c], results[c] = after(got[c], results[c])
            advance(level, c)
    shared = (weights, far_weights, queries, far_queries)
    far_total, gap, far_gap = [None] * CHUNKS, [None] * CHUNKS, [None] * CHUNKS
    for c in chunks:
        total[c], far_total[c], gap[c], far_gap[c] = add_levels((0, 1, 2), c, *shared, total[c], kept[c], *history[c])
        got[c], total[c] = after(got[c], total[c])
        advance(3, c)
    done, parts = [None] * CHUNKS, [None] * CHUNKS
    for c in chunks:
        total[c], far_total[c], gap[c], far_gap[c] = add_levels(
            (3,), c, *shared, total[c], far_total[c], gap[c], far_gap[c], history[c][3]
        )
        got[c], total[c] = after(got[c], total[c])
        part = add_last(c, far_weights, far_queries, far_total[c], far_gap[c], got[c])
        parts[c] = swap(part, 1)
        late, _ = after(got[c], part)
        done[c] = add_last(c, weights, queries, total[c], gap[c], late)
        parts[c], done[c] = after(parts[c], done[c])
    out, = call(
        finish_kernel, [jax.ShapeDtypeStruct((TOK, HEADS * HEAD), BF16)], [*done, *rest, *parts], "finish",
        TOK * CHUNKS * WIDTH, kept=range(3 * CHUNKS), out_specs=[ANY],
        scratch=[pltpu.VMEM((CHUNKS, TOK, WIDTH), BF16), pltpu.SemaphoreType.DMA((2 * CHUNKS,))],
    )
    return out


def solution(mesh):
    placed = (
        P(("seq", "ctx"), None),
        P(("seq", "ctx"), None),
        P(("seq", "ctx"), None),
        P(None, ("seq", "ctx")),
        P(None, None, ("seq", "ctx")),
    )
    return jax.shard_map(
        body, mesh=mesh, in_specs=placed, out_specs=P(("seq", "ctx"), None), check_vma=False
    )
```

```python
import functools

import jax
import jax.numpy as jnp
from jax import lax
from jax.experimental import pallas as pl
from jax.experimental.pallas import tpu as pltpu
from jax.sharding import PartitionSpec as P

HEADS = 32
HEAD = 64
STATE = 128
TOK = 256
LEVELS = 5
SHARE = HEADS // 2
CHUNKS = 2
PAIRS = SHARE // 2 // CHUNKS
WIDTH = PAIRS * 128
BODY = PAIRS * STATE
PACK = BODY + 16
LOG2E = 1.4426950408889634
F32 = jnp.float32
BF16 = jnp.bfloat16
VMEM = pl.BlockSpec(memory_space=pltpu.VMEM)
ANY = pl.BlockSpec(memory_space=pl.ANY)
KEPT = pltpu.MemorySpace.VMEM
PACKET = pltpu.VMEM((PACK, 128), BF16)
SUMS = pltpu.VMEM((8, 128), F32)
TABLE = pltpu.VMEM((TOK, 128), F32)
PART = pltpu.VMEM((TOK, WIDTH), F32)
X_PART = pltpu.VMEM((2, TOK, WIDTH), BF16)


def split3(value):
    high = value.astype(BF16)
    rest = value - high.astype(F32)
    middle = rest.astype(BF16)
    low = (rest - middle.astype(F32)).astype(BF16)
    return high, middle, low


def exact_dot(zero_one, value, dims):
    return sum(
        lax.dot_general(zero_one, part, (dims, ((), ())), preferred_element_type=F32) for part in split3(value)
    )


def pad_heads(value):
    return jnp.concatenate([value, jnp.zeros((128 - HEADS, value.shape[1]), F32)], axis=0)


def spread(table, first):
    lane = lax.broadcasted_iota(jnp.int32, table.shape, 1)
    return jnp.take_along_axis(table, jnp.where(lane < HEAD, first, first + 1), axis=1)


def triangle(compare):
    rows = lax.broadcasted_iota(jnp.int32, (TOK, TOK), 0)
    columns = lax.broadcasted_iota(jnp.int32, (TOK, TOK), 1)
    return compare(rows, columns).astype(F32).astype(BF16)


def total_rows(sums):
    row = lax.broadcasted_iota(jnp.int32, sums.shape, 0)
    high, middle, low = (part.astype(F32) for part in split3(sums))
    rows = jnp.where(row == 0, high, jnp.where(row == 1, middle, jnp.where(row == 2, low, 0.0)))
    return rows.astype(BF16)


def read_total(rows):
    return jnp.sum(rows.astype(F32), axis=0, keepdims=True)


def position():
    index = lax.axis_index("ctx")
    return [(index >> bit) & 1 for bit in range(LEVELS)]


def call(kernel, outs, arrays, name, flops, exps=0, kept=(), far=(), out_specs=None, scratch=(), aliases=None):
    arrays = list(arrays)
    for place in kept:
        arrays[place] = pltpu.with_memory_space_constraint(arrays[place], KEPT)
    for place in far:
        arrays[place] = pltpu.with_memory_space_constraint(arrays[place], pltpu.MemorySpace.HBM)
    return pl.pallas_call(
        kernel,
        out_shape=outs,
        in_specs=[ANY if place in far else VMEM for place in range(len(arrays))],
        out_specs=out_specs or [VMEM] * len(outs),
        scratch_shapes=list(scratch),
        input_output_aliases=aliases or {},
        compiler_params=pltpu.CompilerParams(vmem_limit_bytes=20 << 20),
        cost_estimate=pl.CostEstimate(flops=flops * 100, bytes_accessed=1 << 10, transcendentals=0),
        name=name,
    )(*arrays)


def ends_kernel(chunk, *refs):
    core = position()[0]
    halves = (1 - core, core)
    if chunk == 0:
        sources, refs = refs[0:5], refs[5:]
        sent_ref, kept_ref, factor_ref, sum_ref = refs[0:4]
        decay_ref, key_ref, query_ref, mix_ref = refs[4:8]
        x_refs, (small, big) = refs[8 : 8 + CHUNKS], refs[8 + CHUNKS :]
        x_ref = x_refs[0]
        copies = [
            pltpu.make_async_copy(source, target, small.at[place])
            for place, (source, target) in enumerate(zip(sources, (decay_ref, key_ref, query_ref, mix_ref)))
        ]
        for part in range(CHUNKS):
            for place, half in enumerate(halves):
                columns = pl.ds(pl.multiple_of(half * (CHUNKS * WIDTH) + part * WIDTH, WIDTH), WIDTH)
                copies.append(
                    pltpu.make_async_copy(sources[4].at[:, columns], x_refs[part].at[place], big.at[2 * part + place])
                )
        for place in (0, 1, *range(4, 4 + 2 * CHUNKS), 2, 3):
            copies[place].start()
        copies[0].wait()
        decay = pad_heads(decay_ref[...])
        after = exact_dot(triangle(lambda r, c: c > r), decay, ((1,), (1,)))
        sums = exact_dot(jnp.ones((16, TOK), BF16), decay, ((1,), (1,)))
        factor = jnp.exp(after)
        factor_ref[...] = factor
        sum_ref[...] = sums
        copies[1].wait()
    else:
        x_ref, key_ref, factor_ref, sum_ref, sent_ref, kept_ref = refs
        factor = factor_ref[...]
        sums = sum_ref[...]
    lane = lax.broadcasted_iota(jnp.int32, sums.shape, 1)
    keys = key_ref[...]
    for place, (half, packet_ref) in enumerate(zip(halves, (sent_ref, kept_ref))):
        packet_ref[BODY:PACK] = total_rows(jnp.take_along_axis(sums, (lane + half * SHARE) & 127, axis=1))
        if chunk == 0:
            copies[4 + place].wait()
        for duo in range(PAIRS // 2):
            pieces = []
            for pair in (2 * duo, 2 * duo + 1):
                x = x_ref[place, :, pair * 128 : pair * 128 + 128].astype(F32)
                pieces.append((x * spread(factor, half * SHARE + (chunk * PAIRS + pair) * 2)).astype(BF16))
            decayed = jnp.concatenate(pieces, axis=1)
            state = lax.dot_general(keys, decayed, (((0,), (0,)), ((), ())), preferred_element_type=F32)
            packet_ref[duo * 256 : duo * 256 + 128] = state[:, 0:128].astype(BF16)
            packet_ref[duo * 256 + 128 : duo * 256 + 256] = state[:, 128:256].astype(BF16)
    if chunk == 0:
        for copy in copies[2:4] + copies[6:]:
            copy.wait()


def merge_kernel(bit, chunk, *refs):
    state_ref = sum_ref = None
    if bit == 0:
        own_ref, got_ref, packet_ref, state_ref, sum_ref = refs
        own_sum = read_total(own_ref[BODY:PACK])
    else:
        own_ref, own_sum_ref, got_ref, packet_ref = refs[:4]
        own_sum = own_sum_ref[0:1]
        if bit < LEVELS - 2:
            state_ref, sum_ref = refs[4:]
    right = position()[bit] == 1
    got_sum = read_total(got_ref[BODY:PACK])
    decay = jnp.broadcast_to(jnp.exp(jnp.where(right, own_sum, got_sum)), (8, 128))
    sums = own_sum + got_sum
    if sum_ref is not None:
        sum_ref[...] = jnp.broadcast_to(sums, (8, 128))
    packet_ref[BODY:PACK] = total_rows(jnp.broadcast_to(sums, (16, 128)))
    for pair in range(PAIRS):
        rows = pl.ds(pair * STATE, STATE)
        own = own_ref[rows].astype(F32)
        got = got_ref[rows].astype(F32)
        factor = spread(decay, 2 * (chunk * PAIRS + pair))[0:1]
        state = jnp.where(right, got, own) * factor + jnp.where(right, own, got)
        if state_ref is not None:
            state_ref[rows] = state
        packet_ref[rows] = state.astype(BF16)


def merge(bit, chunk, *arrays):
    outs = [PACKET] + ([pltpu.VMEM((BODY, 128), F32), SUMS] if bit < LEVELS - 2 else [])
    return call(
        functools.partial(merge_kernel, bit, chunk), outs, arrays, "merge", 1 << 19, 4096, range(len(arrays))
    )


def tables_kernel(decay_ref, mix_ref, key_ref, query_ref, scores_ref, column_ref, row_ref, own_ref, sent_ref):
    bits = position()
    core = bits[0]
    decay = decay_ref[...]
    causal = triangle(lambda r, c: r >= c)
    cum_column = exact_dot(causal, pad_heads(decay), ((1,), (1,)))
    cum_row = cum_column.T[0:HEADS]
    row_ref[...] = cum_row * LOG2E
    mix = jnp.concatenate([mix_ref[0], jnp.ones((128 - HEADS, TOK), F32)], axis=0)
    column_ref[...] = (cum_column + jnp.log(mix).T) * LOG2E
    gate = jnp.exp(cum_row)
    weights = [mix_ref[level + 1] * gate * bits[level].astype(F32) for level in range(LEVELS)]
    unused = [jnp.zeros((128 - SHARE * LEVELS, TOK), F32)]
    low = jnp.concatenate([weight[:SHARE] for weight in weights] + unused, axis=0).T
    high = jnp.concatenate([weight[SHARE:] for weight in weights] + unused, axis=0).T
    own_ref[...] = jnp.where(core == 0, low, high)
    queries = query_ref[...]
    sent_ref[:, 0:128] = queries
    far = jnp.where(core == 0, high, low)
    far_high = far.astype(BF16)
    sent_ref[:, 128:256] = far_high
    sent_ref[:, 256:384] = (far - far_high.astype(F32)).astype(BF16)
    raw = lax.dot_general(queries, key_ref[...], (((1,), (1,)), ((), ())), preferred_element_type=F32)
    scores_ref[...] = raw * causal.astype(F32)


def local_kernel(place, chunk, scores_ref, column_ref, row_ref, x_ref, total_ref):
    core = position()[0]
    half = core if place == 1 else 1 - core
    upper = TOK // 2
    lane = lax.broadcasted_iota(jnp.int32, (TOK, 128), 1)

    def pair_step(pair, _):
        offset = pl.multiple_of(pair * 128, 128)
        x = x_ref[place, :, pl.ds(offset, 128)]
        top = jnp.zeros((upper, 128), F32)
        bottom = jnp.zeros((upper, 128), F32)
        for side in range(2):
            head = half * SHARE + (chunk * PAIRS + pair) * 2 + side
            column = jnp.take_along_axis(column_ref[...], jnp.full((TOK, 128), head, jnp.int32), axis=1)
            row = row_ref[pl.ds(head, 1)]
            chosen = jnp.where((lane < HEAD) == (side == 0), x, jnp.zeros_like(x))
            gap = column[:upper] - row[:, :upper]
            mixing = (scores_ref[:upper, :upper] * jnp.exp2(jnp.minimum(gap, 1.0))).astype(BF16)
            top = top + jnp.dot(mixing, chosen[:upper], preferred_element_type=F32)
            below = column[upper:]
            gap = jnp.concatenate([below, below], axis=1) - row
            mixing = (scores_ref[upper:] * jnp.exp2(jnp.minimum(gap, 1.0))).astype(BF16)
            bottom = bottom + jnp.dot(mixing, chosen, preferred_element_type=F32)
        total_ref[:upper, pl.ds(offset, 128)] = top
        total_ref[upper:, pl.ds(offset, 128)] = bottom
        return 0

    lax.fori_loop(0, PAIRS, pair_step, 0, unroll=True)


def make_local(place, chunk, *arrays):
    return call(
        functools.partial(local_kernel, place, chunk), [PART], arrays, "local", 4 * TOK * TOK * WIDTH,
        2 * PAIRS * TOK * TOK, kept=range(4),
    )[0]


def duo_columns(packet_ref, duo):
    rows = duo * 256
    return jnp.concatenate([packet_ref[rows : rows + 128], packet_ref[rows + 128 : rows + 256]], axis=1)


def duo_spread(table, first):
    return jnp.concatenate([spread(table, first), spread(table, first + 2)], axis=1)


def far_tables(far_ref):
    return far_ref[:, 0:128], far_ref[:, 128:256].astype(F32) + far_ref[:, 256:384].astype(F32)


def level_term(level, chunk, duo, queries, packet_ref, weights, gap):
    product = jnp.dot(queries, duo_columns(packet_ref, duo), preferred_element_type=F32)
    pair = chunk * PAIRS + duo * 2
    return product * (duo_spread(weights, level * SHARE + pair * 2) * duo_spread(gap, pair * 2)[0:1])


def levels_kernel(wanted, chunk, *refs):
    bits = position()
    own, far = (refs[0][...], refs[1][...]), far_tables(refs[2])
    refs = refs[3:]
    if wanted[0] == 0:
        total_ref, kept_ref, *packets = refs[:-4]
        totals = (total_ref, None)
        gaps = [jnp.zeros((8, 128), F32)] * 2
    else:
        totals, gaps, packets = refs[0:2], [refs[2][...], refs[3][...]], refs[4:-4]
        kept_ref = None
    outs, gap_outs = refs[-4:-2], refs[-2:]
    for side in range(2):
        queries, weights = far if side else own
        used = [kept_ref if side == 1 and level == 0 else packet for level, packet in zip(wanted, packets)]
        gap, before = gaps[side], []
        for level, packet in zip(wanted, used):
            before.append(jnp.exp(gap))
            bit = 1 - bits[0] if side == 1 and level == 0 else bits[level]
            gap = gap + read_total(packet[BODY:PACK]) * bit.astype(F32)
        gap_outs[side][...] = gap
        for duo in range(PAIRS // 2):
            lanes = slice(duo * 256, duo * 256 + 256)
            running = None if totals[side] is None else totals[side][:, lanes]
            for level, packet, factor in zip(wanted, used, before):
                term = level_term(level, chunk, duo, queries, packet, weights, factor)
                running = term if running is None else running + term
            outs[side][:, lanes] = running


def add_levels(wanted, chunk, *arrays):
    return call(
        functools.partial(levels_kernel, wanted, chunk), [PART, PART, SUMS, SUMS], arrays, "levels",
        4 * len(wanted) * TOK * STATE * WIDTH, kept=range(len(arrays)),
    )


def last_kernel(far, chunk, *refs):
    if far:
        queries, weights = far_tables(refs[0])
    else:
        queries, weights = refs[0][...], refs[1][...]
    total_ref, gap_ref, packet_ref, out_ref = refs[-4:]
    gap = jnp.exp(gap_ref[...])
    for duo in range(PAIRS // 2):
        lanes = slice(duo * 256, duo * 256 + 256)
        term = level_term(LEVELS - 1, chunk, duo, queries, packet_ref, weights, gap)
        out_ref[:, lanes] = (total_ref[:, lanes] + term).astype(BF16)


def add_last(far, chunk, *arrays):
    return call(
        functools.partial(last_kernel, far, chunk), [pltpu.VMEM((TOK, WIDTH), BF16)], arrays, "last",
        2 * TOK * STATE * WIDTH, kept=range(len(arrays)),
    )[0]


def finish_kernel(*refs):
    done, totals, parts = refs[:CHUNKS], refs[CHUNKS : 2 * CHUNKS], refs[2 * CHUNKS : 3 * CHUNKS]
    out_ref, buffer, sems = refs[3 * CHUNKS :]
    core = position()[0]
    copies = []

    def send(source, half, chunk):
        columns = pl.ds(pl.multiple_of(half * (CHUNKS * WIDTH) + chunk * WIDTH, WIDTH), WIDTH)
        copies.append(pltpu.make_async_copy(source, out_ref.at[:, columns], sems.at[len(copies)]))
        copies[-1].start()

    for chunk in range(CHUNKS):
        send(done[chunk], core, chunk)
    for chunk in range(CHUNKS):
        buffer[chunk] = (totals[chunk][...] + parts[chunk][...].astype(F32)).astype(BF16)
        send(buffer.at[chunk], 1 - core, chunk)
    for copy in copies:
        copy.wait()


def body(inputs, write_keys, read_queries, decay_log, level_mix):
    devices = lax.axis_size("ctx")

    def swap(array, mask):
        return lax.ppermute(array, "ctx", [(i, i ^ mask) for i in range(devices)])

    def after(*arrays):
        return lax.optimization_barrier(arrays)

    chunks = range(CHUNKS)
    masks = (1, 2, 6, 8, 24)
    kept, x, got, state, packet = ([None] * CHUNKS for _ in range(5))
    history = [[] for _ in chunks]
    for c in chunks:
        kernel, flops = functools.partial(ends_kernel, c), 4 * TOK * STATE * WIDTH
        if c == 0:
            sent, kept[c], factor, sums, decay, keys, queries, mix, *x = call(
                kernel,
                [
                    PACKET, PACKET, TABLE, pltpu.VMEM((16, 128), F32), pltpu.VMEM((HEADS, TOK), F32),
                    pltpu.VMEM((TOK, STATE), BF16), pltpu.VMEM((TOK, STATE), BF16),
                    pltpu.VMEM((LEVELS + 1, HEADS, TOK), F32),
                ] + [X_PART] * CHUNKS,
                [decay_log, write_keys, read_queries, level_mix, inputs], "ends", flops, 32768, far=range(5),
                scratch=[pltpu.SemaphoreType.DMA((4,)), pltpu.SemaphoreType.DMA((2 * CHUNKS,))],
            )
        else:
            sent, kept[c] = call(
                kernel, [PACKET, PACKET], [x[c], keys, factor, sums], "ends", flops, kept=range(4)
            )
            got[c - 1], sent = after(got[c - 1], sent)
        got[c] = swap(sent, masks[0])

    def advance(level, c):
        if c > 0:
            got[c], _ = after(got[c], packet[c - 1])
        history[c].append(got[c])
        if level == 0:
            packet[c], *state[c] = merge(0, c, kept[c], got[c])
        else:
            packet[c], *state[c] = merge(level, c, *state[c], got[c])
        got[c] = swap(packet[c], masks[level + 1])

    for c in chunks:
        advance(0, c)
    queries, mix, _ = after(queries, mix, packet[-1])
    scores, column, row, weights, tables = call(
        tables_kernel,
        [
            pltpu.VMEM((TOK, TOK), F32), TABLE, pltpu.VMEM((HEADS, TOK), F32), TABLE, pltpu.VMEM((TOK, 384), BF16),
        ],
        [decay, mix, keys, queries], "tables", 4 * TOK * TOK * STATE, 16384, kept=range(4),
    )
    far = swap(tables, 1)
    total, rest = [None] * CHUNKS, [None] * CHUNKS
    for level, place, results in ((1, 1, total), (2, 0, rest)):
        for c in chunks:
            if c > 0:
                x[c], _ = after(x[c], packet[c - 1])
            results[c] = make_local(place, c, scores, column, row, x[c])
            got[c], results[c], far = after(got[c], results[c], far)
            advance(level, c)
    shared = (queries, weights, far)
    far_total, gap, far_gap = [None] * CHUNKS, [None] * CHUNKS, [None] * CHUNKS
    for c in chunks:
        if c > 0:
            total[c], _ = after(total[c], packet[c - 1])
        total[c], far_total[c], gap[c], far_gap[c] = add_levels((0, 1, 2), c, *shared, total[c], kept[c], *history[c])
        got[c], total[c] = after(got[c], total[c])
        advance(3, c)
    done, parts = [None] * CHUNKS, [None] * CHUNKS
    for c in chunks:
        total[c], far_total[c], gap[c], far_gap[c] = add_levels(
            (3,), c, *shared, total[c], far_total[c], gap[c], far_gap[c], history[c][3]
        )
        got[c], total[c] = after(got[c], total[c])
        part = add_last(True, c, far, far_total[c], far_gap[c], got[c])
        parts[c] = swap(part, 1)
        late, _ = after(got[c], part)
        done[c] = add_last(False, c, queries, weights, total[c], gap[c], late)
        parts[c], done[c] = after(parts[c], done[c])
    out, = call(
        finish_kernel, [jax.ShapeDtypeStruct((TOK, HEADS * HEAD), BF16)], [*done, *rest, *parts], "finish",
        TOK * CHUNKS * WIDTH, kept=range(3 * CHUNKS), out_specs=[ANY],
        scratch=[pltpu.VMEM((CHUNKS, TOK, WIDTH), BF16), pltpu.SemaphoreType.DMA((2 * CHUNKS,))],
    )
    return out


def solution(mesh):
    placed = (
        P(("seq", "ctx"), None),
        P(("seq", "ctx"), None),
        P(("seq", "ctx"), None),
        P(None, ("seq", "ctx")),
        P(None, None, ("seq", "ctx")),
    )
    return jax.shard_map(
        body, mesh=mesh, in_specs=placed, out_specs=P(("seq", "ctx"), None), check_vma=False
    )
```

```python
import functools

import jax
import jax.numpy as jnp
from jax import lax
from jax.experimental import pallas as pl
from jax.experimental.pallas import tpu as pltpu
from jax.sharding import PartitionSpec as P

HEADS = 32
HEAD = 64
STATE = 128
TOK = 256
LEVELS = 5
SHARE = HEADS // 2
CHUNKS = 2
PAIRS = SHARE // 2 // CHUNKS
WIDTH = PAIRS * 128
BODY = PAIRS * STATE
PACK = BODY + 16
LOG2E = 1.4426950408889634
F32 = jnp.float32
BF16 = jnp.bfloat16
VMEM = pl.BlockSpec(memory_space=pltpu.VMEM)
ANY = pl.BlockSpec(memory_space=pl.ANY)
KEPT = pltpu.MemorySpace.VMEM
PACKET = pltpu.VMEM((PACK, 128), BF16)
SUMS = pltpu.VMEM((8, 128), F32)
TABLE = pltpu.VMEM((TOK, 128), F32)
PART = pltpu.VMEM((TOK, WIDTH), F32)
X_PART = pltpu.VMEM((2, TOK, WIDTH), BF16)


def split3(value):
    high = value.astype(BF16)
    rest = value - high.astype(F32)
    middle = rest.astype(BF16)
    low = (rest - middle.astype(F32)).astype(BF16)
    return high, middle, low


def exact_dot(zero_one, value, dims, terms=2):
    return sum(
        lax.dot_general(zero_one, part, (dims, ((), ())), preferred_element_type=F32)
        for part in split3(value)[:terms]
    )


def pad_heads(value):
    return jnp.concatenate([value, jnp.zeros((128 - HEADS, value.shape[1]), F32)], axis=0)


def spread(table, first):
    lane = lax.broadcasted_iota(jnp.int32, table.shape, 1)
    return jnp.take_along_axis(table, jnp.where(lane < HEAD, first, first + 1), axis=1)


def triangle(compare):
    rows = lax.broadcasted_iota(jnp.int32, (TOK, TOK), 0)
    columns = lax.broadcasted_iota(jnp.int32, (TOK, TOK), 1)
    return compare(rows, columns).astype(F32).astype(BF16)


def total_rows(sums):
    row = lax.broadcasted_iota(jnp.int32, sums.shape, 0)
    high, middle, low = (part.astype(F32) for part in split3(sums))
    rows = jnp.where(row == 0, high, jnp.where(row == 1, middle, jnp.where(row == 2, low, 0.0)))
    return rows.astype(BF16)


def read_total(rows):
    return jnp.sum(rows.astype(F32), axis=0, keepdims=True)


def position():
    index = lax.axis_index("ctx")
    return [(index >> bit) & 1 for bit in range(LEVELS)]


def call(kernel, outs, arrays, name, flops, exps=0, kept=(), far=(), out_specs=None, scratch=(), aliases=None):
    arrays = list(arrays)
    for place in kept:
        arrays[place] = pltpu.with_memory_space_constraint(arrays[place], KEPT)
    for place in far:
        arrays[place] = pltpu.with_memory_space_constraint(arrays[place], pltpu.MemorySpace.HBM)
    return pl.pallas_call(
        kernel,
        out_shape=outs,
        in_specs=[ANY if place in far else VMEM for place in range(len(arrays))],
        out_specs=out_specs or [VMEM] * len(outs),
        scratch_shapes=list(scratch),
        input_output_aliases=aliases or {},
        compiler_params=pltpu.CompilerParams(vmem_limit_bytes=20 << 20),
        cost_estimate=pl.CostEstimate(flops=flops * 100, bytes_accessed=1 << 10, transcendentals=0),
        name=name,
    )(*arrays)


def fill_packet(place, chunk, x_ref, keys, factor, sums, packet_ref):
    core = position()[0]
    first = (core if place == 1 else 1 - core) * SHARE
    lane = lax.broadcasted_iota(jnp.int32, sums.shape, 1)
    packet_ref[BODY:PACK] = total_rows(jnp.take_along_axis(sums, (lane + first) & 127, axis=1))
    for duo in range(PAIRS // 2):
        pieces = []
        for pair in (2 * duo, 2 * duo + 1):
            x = x_ref[place, :, pair * 128 : pair * 128 + 128].astype(F32)
            pieces.append((x * spread(factor, first + (chunk * PAIRS + pair) * 2)).astype(BF16))
        decayed = jnp.concatenate(pieces, axis=1)
        state = lax.dot_general(keys, decayed, (((0,), (0,)), ((), ())), preferred_element_type=F32)
        packet_ref[duo * 256 : duo * 256 + 128] = state[:, 0:128].astype(BF16)
        packet_ref[duo * 256 + 128 : duo * 256 + 256] = state[:, 128:256].astype(BF16)


def fetch_kernel(*refs):
    sources, sent_ref, factor_ref, sum_ref = refs[0:5], *refs[5:8]
    targets, x_refs, (small, big) = refs[8:12], refs[12 : 12 + CHUNKS], refs[12 + CHUNKS :]
    core = position()[0]
    copies = [
        pltpu.make_async_copy(source, target, small.at[place])
        for place, (source, target) in enumerate(zip(sources, targets))
    ]
    for chunk in range(CHUNKS):
        for place, half in enumerate((1 - core, core)):
            columns = pl.ds(pl.multiple_of(half * (CHUNKS * WIDTH) + chunk * WIDTH, WIDTH), WIDTH)
            copies.append(
                pltpu.make_async_copy(sources[4].at[:, columns], x_refs[chunk].at[place], big.at[2 * chunk + place])
            )
    for place in (0, 4, 1, *range(5, 4 + 2 * CHUNKS), 2, 3):
        copies[place].start()
    later = triangle(lambda r, c: c > r)
    copies[0].wait()
    decay = pad_heads(targets[0][...])
    factor = jnp.exp(exact_dot(later, decay, ((1,), (1,))))
    sums = exact_dot(jnp.ones((16, TOK), BF16), decay, ((1,), (1,)), 3)
    factor_ref[...] = factor
    sum_ref[...] = sums
    copies[1].wait()
    copies[4].wait()
    fill_packet(0, 0, x_refs[0], targets[1][...], factor, sums, sent_ref)
    for copy in copies[2:4] + copies[5:]:
        copy.wait()


def ends_kernel(place, chunk, x_ref, key_ref, factor_ref, sum_ref, packet_ref):
    fill_packet(place, chunk, x_ref, key_ref[...], factor_ref[...], sum_ref[...], packet_ref)


def make_ends(place, chunk, *arrays):
    return call(
        functools.partial(ends_kernel, place, chunk), [PACKET], arrays, "ends", 2 * TOK * STATE * WIDTH, kept=range(4)
    )[0]


def merge_kernel(bit, chunk, *refs):
    state_ref = sum_ref = None
    if bit == 0:
        own_ref, got_ref, packet_ref, state_ref, sum_ref = refs
        own_sum = read_total(own_ref[BODY:PACK])
    else:
        own_ref, own_sum_ref, got_ref, packet_ref = refs[:4]
        own_sum = own_sum_ref[0:1]
        if bit < LEVELS - 2:
            state_ref, sum_ref = refs[4:]
    right = position()[bit] == 1
    got_sum = read_total(got_ref[BODY:PACK])
    decay = jnp.broadcast_to(jnp.exp(jnp.where(right, own_sum, got_sum)), (8, 128))
    sums = own_sum + got_sum
    if sum_ref is not None:
        sum_ref[...] = jnp.broadcast_to(sums, (8, 128))
    packet_ref[BODY:PACK] = total_rows(jnp.broadcast_to(sums, (16, 128)))
    for pair in range(PAIRS):
        rows = pl.ds(pair * STATE, STATE)
        own = own_ref[rows].astype(F32)
        got = got_ref[rows].astype(F32)
        factor = spread(decay, 2 * (chunk * PAIRS + pair))[0:1]
        state = jnp.where(right, got, own) * factor + jnp.where(right, own, got)
        if state_ref is not None:
            state_ref[rows] = state
        packet_ref[rows] = state.astype(BF16)


def merge(bit, chunk, *arrays):
    outs = [PACKET] + ([pltpu.VMEM((BODY, 128), F32), SUMS] if bit < LEVELS - 2 else [])
    return call(
        functools.partial(merge_kernel, bit, chunk), outs, arrays, "merge", 1 << 19, 4096, range(len(arrays))
    )


def tables_kernel(decay_ref, mix_ref, key_ref, query_ref, scores_ref, column_ref, row_ref, own_ref, sent_ref):
    bits = position()
    core = bits[0]
    decay = decay_ref[...]
    causal = triangle(lambda r, c: r >= c)
    cum_column = exact_dot(causal, pad_heads(decay), ((1,), (1,)))
    cum_row = cum_column.T[0:HEADS]
    row_ref[...] = cum_row * LOG2E
    mix = jnp.concatenate([mix_ref[0], jnp.ones((128 - HEADS, TOK), F32)], axis=0)
    column_ref[...] = (cum_column + jnp.log(mix).T) * LOG2E
    gate = jnp.exp(cum_row)
    weights = [mix_ref[level + 1] * gate * bits[level].astype(F32) for level in range(LEVELS)]
    unused = [jnp.zeros((128 - SHARE * LEVELS, TOK), F32)]
    low = jnp.concatenate([weight[:SHARE] for weight in weights] + unused, axis=0).T
    high = jnp.concatenate([weight[SHARE:] for weight in weights] + unused, axis=0).T
    own_ref[...] = jnp.where(core == 0, low, high)
    queries = query_ref[...]
    sent_ref[:, 0:128] = queries
    far = jnp.where(core == 0, high, low)
    far_high = far.astype(BF16)
    sent_ref[:, 128:256] = far_high
    sent_ref[:, 256:384] = (far - far_high.astype(F32)).astype(BF16)
    raw = lax.dot_general(queries, key_ref[...], (((1,), (1,)), ((), ())), preferred_element_type=F32)
    scores_ref[...] = raw * causal.astype(F32)


def local_kernel(place, chunk, scores_ref, column_ref, row_ref, x_ref, total_ref):
    core = position()[0]
    half = core if place == 1 else 1 - core
    upper = TOK // 2
    lane = lax.broadcasted_iota(jnp.int32, (TOK, 128), 1)

    def pair_step(pair, _):
        offset = pl.multiple_of(pair * 128, 128)
        x = x_ref[place, :, pl.ds(offset, 128)]
        top = jnp.zeros((upper, 128), F32)
        bottom = jnp.zeros((upper, 128), F32)
        for side in range(2):
            head = half * SHARE + (chunk * PAIRS + pair) * 2 + side
            column = jnp.take_along_axis(column_ref[...], jnp.full((TOK, 128), head, jnp.int32), axis=1)
            row = row_ref[pl.ds(head, 1)]
            chosen = jnp.where((lane < HEAD) == (side == 0), x, jnp.zeros_like(x))
            gap = column[:upper] - row[:, :upper]
            mixing = (scores_ref[:upper, :upper] * jnp.exp2(jnp.minimum(gap, 1.0))).astype(BF16)
            top = top + jnp.dot(mixing, chosen[:upper], preferred_element_type=F32)
            below = column[upper:]
            gap = jnp.concatenate([below, below], axis=1) - row
            mixing = (scores_ref[upper:] * jnp.exp2(jnp.minimum(gap, 1.0))).astype(BF16)
            bottom = bottom + jnp.dot(mixing, chosen, preferred_element_type=F32)
        total_ref[:upper, pl.ds(offset, 128)] = top
        total_ref[upper:, pl.ds(offset, 128)] = bottom
        return 0

    lax.fori_loop(0, PAIRS, pair_step, 0, unroll=True)


def make_local(place, chunk, *arrays):
    return call(
        functools.partial(local_kernel, place, chunk), [PART], arrays, "local", 4 * TOK * TOK * WIDTH,
        2 * PAIRS * TOK * TOK, kept=range(4),
    )[0]


def duo_columns(packet_ref, duo):
    rows = duo * 256
    return jnp.concatenate([packet_ref[rows : rows + 128], packet_ref[rows + 128 : rows + 256]], axis=1)


def duo_spread(table, first):
    return jnp.concatenate([spread(table, first), spread(table, first + 2)], axis=1)


def far_tables(far_ref):
    return far_ref[:, 0:128], far_ref[:, 128:256].astype(F32) + far_ref[:, 256:384].astype(F32)


def level_term(level, chunk, duo, queries, packet_ref, weights, gap):
    product = jnp.dot(queries, duo_columns(packet_ref, duo), preferred_element_type=F32)
    pair = chunk * PAIRS + duo * 2
    return product * (duo_spread(weights, level * SHARE + pair * 2) * duo_spread(gap, pair * 2)[0:1])


def levels_kernel(wanted, chunk, *refs):
    bits = position()
    own, far = (refs[0][...], refs[1][...]), far_tables(refs[2])
    refs = refs[3:]
    if wanted[0] == 0:
        total_ref, kept_ref, *packets = refs[:-4]
        totals = (total_ref, None)
        gaps = [jnp.zeros((8, 128), F32)] * 2
    else:
        totals, gaps, packets = refs[0:2], [refs[2][...], refs[3][...]], refs[4:-4]
        kept_ref = None
    outs, gap_outs = refs[-4:-2], refs[-2:]
    for side in range(2):
        queries, weights = far if side else own
        used = [kept_ref if side == 1 and level == 0 else packet for level, packet in zip(wanted, packets)]
        gap, before = gaps[side], []
        for level, packet in zip(wanted, used):
            before.append(jnp.exp(gap))
            bit = 1 - bits[0] if side == 1 and level == 0 else bits[level]
            gap = gap + read_total(packet[BODY:PACK]) * bit.astype(F32)
        gap_outs[side][...] = gap
        for duo in range(PAIRS // 2):
            lanes = slice(duo * 256, duo * 256 + 256)
            running = None if totals[side] is None else totals[side][:, lanes]
            for level, packet, factor in zip(wanted, used, before):
                term = level_term(level, chunk, duo, queries, packet, weights, factor)
                running = term if running is None else running + term
            outs[side][:, lanes] = running


def add_levels(wanted, chunk, *arrays):
    return call(
        functools.partial(levels_kernel, wanted, chunk), [PART, PART, SUMS, SUMS], arrays, "levels",
        4 * len(wanted) * TOK * STATE * WIDTH, kept=range(len(arrays)),
    )


def last_kernel(far, chunk, *refs):
    if far:
        queries, weights = far_tables(refs[0])
    else:
        queries, weights = refs[0][...], refs[1][...]
    total_ref, gap_ref, packet_ref, out_ref = refs[-4:]
    gap = jnp.exp(gap_ref[...])
    for duo in range(PAIRS // 2):
        lanes = slice(duo * 256, duo * 256 + 256)
        term = level_term(LEVELS - 1, chunk, duo, queries, packet_ref, weights, gap)
        out_ref[:, lanes] = (total_ref[:, lanes] + term).astype(BF16)


def add_last(far, chunk, *arrays):
    return call(
        functools.partial(last_kernel, far, chunk), [pltpu.VMEM((TOK, WIDTH), BF16)], arrays, "last",
        2 * TOK * STATE * WIDTH, kept=range(len(arrays)),
    )[0]


def finish_kernel(first, *refs):
    out_ref, buffer, sems = refs[-3:]
    core = position()[0]
    copies = []

    def send(source, half, chunk, start, width):
        columns = pl.ds(pl.multiple_of(half * (CHUNKS * WIDTH) + chunk * WIDTH + start, 256), width)
        copies.append(pltpu.make_async_copy(source, out_ref.at[:, columns], sems.at[len(copies)]))
        copies[-1].start()

    if first:
        for chunk in range(CHUNKS):
            send(refs[chunk], core, chunk, 0, WIDTH)
        rest_ref, part_ref, chunk = refs[CHUNKS], refs[CHUNKS + 1], 0
    else:
        rest_ref, part_ref, chunk = refs[0], refs[1], CHUNKS - 1
    for piece in range(WIDTH // 256):
        lanes = slice(piece * 256, piece * 256 + 256)
        buffer[piece] = (rest_ref[:, lanes] + part_ref[:, lanes].astype(F32)).astype(BF16)
        send(buffer.at[piece], 1 - core, chunk, piece * 256, 256)
    for copy in copies:
        copy.wait()


def finish(first, arrays, out=None):
    count = len(arrays)
    return call(
        functools.partial(finish_kernel, first), [jax.ShapeDtypeStruct((TOK, HEADS * HEAD), BF16)],
        [*arrays] if first else [*arrays, out], "finish", TOK * WIDTH, kept=range(count),
        far=() if first else (count,), out_specs=[ANY], aliases=None if first else {count: 0},
        scratch=[pltpu.VMEM((WIDTH // 256, TOK, 256), BF16), pltpu.SemaphoreType.DMA((CHUNKS + WIDTH // 256,))],
    )[0]


def body(inputs, write_keys, read_queries, decay_log, level_mix):
    devices = lax.axis_size("ctx")

    def swap(array, mask, senders=None):
        return lax.ppermute(array, "ctx", [(i, i ^ mask) for i in range(senders or devices)])

    def after(*arrays):
        return lax.optimization_barrier(arrays)

    chunks = range(CHUNKS)
    masks = (1, 2, 6, 8, 24)
    kept, x, got, state, packet = ([None] * CHUNKS for _ in range(5))
    history = [[] for _ in chunks]
    sent, factor, sums, decay, keys, queries, mix, *x = call(
        fetch_kernel,
        [
            PACKET, TABLE, pltpu.VMEM((16, 128), F32), pltpu.VMEM((HEADS, TOK), F32), pltpu.VMEM((TOK, STATE), BF16),
            pltpu.VMEM((TOK, STATE), BF16), pltpu.VMEM((LEVELS + 1, HEADS, TOK), F32),
        ] + [X_PART] * CHUNKS,
        [decay_log, write_keys, read_queries, level_mix, inputs], "fetch", 2 * TOK * STATE * WIDTH, far=range(5),
        scratch=[pltpu.SemaphoreType.DMA((4,)), pltpu.SemaphoreType.DMA((2 * CHUNKS,))],
    )
    got[0] = swap(sent, masks[0])
    for c in chunks[1:]:
        sent = make_ends(0, c, x[c], keys, factor, sums)
        got[c] = swap(sent, masks[0])
    x[0], _ = after(x[0], sent)
    kept[0] = make_ends(1, 0, x[0], keys, factor, sums)

    def advance(level, c):
        if c > 0:
            got[c], _ = after(got[c], packet[c - 1])
            if level == 0:
                x[c], _ = after(x[c], packet[c - 1])
                kept[c] = make_ends(1, c, x[c], keys, factor, sums)
        history[c].append(got[c])
        if level == 0:
            packet[c], *state[c] = merge(0, c, kept[c], got[c])
        else:
            packet[c], *state[c] = merge(level, c, *state[c], got[c])
        got[c] = swap(packet[c], masks[level + 1], devices // 2 if level == 3 and c in (0, 1) else None)

    for c in chunks:
        advance(0, c)
    queries, mix, _ = after(queries, mix, packet[-1])
    scores, column, row, weights, tables = call(
        tables_kernel,
        [
            pltpu.VMEM((TOK, TOK), F32), TABLE, pltpu.VMEM((HEADS, TOK), F32), TABLE, pltpu.VMEM((TOK, 384), BF16),
        ],
        [decay, mix, keys, queries], "tables", 4 * TOK * TOK * STATE, 16384, kept=range(4),
    )
    far = swap(tables, 1)
    local = (scores, column, row)
    levels = [None] * CHUNKS

    def add(wanted, c):
        arrays = [*levels[c], *(history[c][level] for level in wanted)]
        levels[c] = add_levels(wanted, c, queries, weights, far, *arrays)

    for c in chunks:
        levels[c] = [make_local(1, c, *local, x[c]), kept[c]]
    got[0], far, *levels = after(got[0], far, *levels)
    for c in chunks:
        advance(1, c)
    rest = [None] * CHUNKS
    x[0], levels[0], _ = after(x[0], levels[0], packet[1])
    add((0, 1), 0)
    rest[0] = make_local(0, 0, *local, x[0])
    got[0], levels[0], rest[0] = after(got[0], levels[0], rest[0])
    for c in chunks:
        advance(2, c)
    x[1], levels[0], levels[1], _ = after(x[1], *levels, packet[1])
    add((0, 1), 1)
    add((2,), 0)
    rest[1] = make_local(0, 1, *local, x[1])
    got[0], levels[0], levels[1], rest[1] = after(got[0], *levels, rest[1])
    for c in chunks:
        advance(3, c)
    levels[0], levels[1], _ = after(*levels, packet[1])
    add((3,), 0)
    add((2, 3), 1)
    got[0], levels[0], levels[1] = after(got[0], *levels)
    done, parts = [None] * CHUNKS, [None] * CHUNKS
    for c in chunks:
        total, far_total, gap, far_gap = levels[c]
        part = add_last(True, c, far, far_total, far_gap, got[c])
        parts[c] = swap(part, 1)
        late, _ = after(got[c], part)
        done[c] = add_last(False, c, queries, weights, total, gap, late)
        if c == 0:
            got[1], done[0] = after(got[1], done[0])
    out = finish(True, [*done, rest[0], parts[0]])
    parts[1], out = after(parts[1], out)
    return finish(False, [rest[1], parts[1]], out)


def solution(mesh):
    placed = (
        P(("seq", "ctx"), None),
        P(("seq", "ctx"), None),
        P(("seq", "ctx"), None),
        P(None, ("seq", "ctx")),
        P(None, None, ("seq", "ctx")),
    )
    return jax.shard_map(
        body, mesh=mesh, in_specs=placed, out_specs=P(("seq", "ctx"), None), check_vma=False
    )
```

```python
import functools

import jax
import jax.numpy as jnp
from jax import lax
from jax.experimental import pallas as pl
from jax.experimental.pallas import tpu as pltpu
from jax.sharding import PartitionSpec as P

HEADS = 32
HEAD = 64
STATE = 128
TOK = 256
LEVELS = 5
SHARE = HEADS // 2
CHUNKS = 2
PAIRS = SHARE // 2 // CHUNKS
WIDTH = PAIRS * 128
BODY = PAIRS * STATE
PACK = BODY + 16
LOG2E = 1.4426950408889634
F32 = jnp.float32
BF16 = jnp.bfloat16
VMEM = pl.BlockSpec(memory_space=pltpu.VMEM)
ANY = pl.BlockSpec(memory_space=pl.ANY)
KEPT = pltpu.MemorySpace.VMEM
PACKET = pltpu.VMEM((PACK, 128), BF16)
SUMS = pltpu.VMEM((8, 128), F32)
TABLE = pltpu.VMEM((TOK, 128), F32)
PART = pltpu.VMEM((TOK, WIDTH), F32)
X_PART = pltpu.VMEM((2, TOK, WIDTH), BF16)


def split3(value):
    high = value.astype(BF16)
    rest = value - high.astype(F32)
    middle = rest.astype(BF16)
    low = (rest - middle.astype(F32)).astype(BF16)
    return high, middle, low


def exact_dot(zero_one, value, dims, terms=2):
    return sum(
        lax.dot_general(zero_one, part, (dims, ((), ())), preferred_element_type=F32)
        for part in split3(value)[:terms]
    )


def pad_heads(value):
    return jnp.concatenate([value, jnp.zeros((128 - HEADS, value.shape[1]), F32)], axis=0)


def spread(table, first):
    lane = lax.broadcasted_iota(jnp.int32, table.shape, 1)
    return jnp.take_along_axis(table, jnp.where(lane < HEAD, first, first + 1), axis=1)


def triangle(compare):
    rows = lax.broadcasted_iota(jnp.int32, (TOK, TOK), 0)
    columns = lax.broadcasted_iota(jnp.int32, (TOK, TOK), 1)
    return compare(rows, columns).astype(F32).astype(BF16)


def total_rows(sums):
    row = lax.broadcasted_iota(jnp.int32, sums.shape, 0)
    high, middle, low = (part.astype(F32) for part in split3(sums))
    rows = jnp.where(row == 0, high, jnp.where(row == 1, middle, jnp.where(row == 2, low, 0.0)))
    return rows.astype(BF16)


def read_total(rows):
    return jnp.sum(rows.astype(F32), axis=0, keepdims=True)


def position():
    index = lax.axis_index("ctx")
    return [(index >> bit) & 1 for bit in range(LEVELS)]


def call(kernel, outs, arrays, name, flops, exps=0, kept=(), far=(), out_specs=None, scratch=(), aliases=None):
    arrays = list(arrays)
    for place in kept:
        arrays[place] = pltpu.with_memory_space_constraint(arrays[place], KEPT)
    for place in far:
        arrays[place] = pltpu.with_memory_space_constraint(arrays[place], pltpu.MemorySpace.HBM)
    return pl.pallas_call(
        kernel,
        out_shape=outs,
        in_specs=[ANY if place in far else VMEM for place in range(len(arrays))],
        out_specs=out_specs or [VMEM] * len(outs),
        scratch_shapes=list(scratch),
        input_output_aliases=aliases or {},
        compiler_params=pltpu.CompilerParams(vmem_limit_bytes=20 << 20),
        cost_estimate=pl.CostEstimate(flops=flops * 100, bytes_accessed=1 << 10, transcendentals=0),
        name=name,
    )(*arrays)


def fill_packet(place, chunk, x_ref, keys, factor, sums, packet_ref):
    core = position()[0]
    first = (core if place == 1 else 1 - core) * SHARE
    lane = lax.broadcasted_iota(jnp.int32, sums.shape, 1)
    packet_ref[BODY:PACK] = total_rows(jnp.take_along_axis(sums, (lane + first) & 127, axis=1))
    for duo in range(PAIRS // 2):
        pieces = []
        for pair in (2 * duo, 2 * duo + 1):
            x = x_ref[place, :, pair * 128 : pair * 128 + 128].astype(F32)
            pieces.append((x * spread(factor, first + (chunk * PAIRS + pair) * 2)).astype(BF16))
        decayed = jnp.concatenate(pieces, axis=1)
        state = lax.dot_general(keys, decayed, (((0,), (0,)), ((), ())), preferred_element_type=F32)
        packet_ref[duo * 256 : duo * 256 + 128] = state[:, 0:128].astype(BF16)
        packet_ref[duo * 256 + 128 : duo * 256 + 256] = state[:, 128:256].astype(BF16)


def fetch_kernel(*refs):
    sources, sent_ref, factor_ref, sum_ref = refs[0:5], *refs[5:8]
    targets, x_refs, (small, big) = refs[8:12], refs[12 : 12 + CHUNKS], refs[12 + CHUNKS :]
    core = position()[0]
    copies = [
        pltpu.make_async_copy(source, target, small.at[place])
        for place, (source, target) in enumerate(zip(sources, targets))
    ]
    for chunk in range(CHUNKS):
        for place, half in enumerate((1 - core, core)):
            columns = pl.ds(pl.multiple_of(half * (CHUNKS * WIDTH) + chunk * WIDTH, WIDTH), WIDTH)
            copies.append(
                pltpu.make_async_copy(sources[4].at[:, columns], x_refs[chunk].at[place], big.at[2 * chunk + place])
            )
    for place in (0, 4, 1, *range(5, 4 + 2 * CHUNKS), 2, 3):
        copies[place].start()
    later = triangle(lambda r, c: c > r)
    copies[0].wait()
    decay = pad_heads(targets[0][...])
    factor = jnp.exp(exact_dot(later, decay, ((1,), (1,))))
    sums = exact_dot(jnp.ones((16, TOK), BF16), decay, ((1,), (1,)), 3)
    factor_ref[...] = factor
    sum_ref[...] = sums
    copies[1].wait()
    copies[4].wait()
    fill_packet(0, 0, x_refs[0], targets[1][...], factor, sums, sent_ref)
    for copy in copies[2:4] + copies[5:]:
        copy.wait()


def ends_kernel(place, chunk, x_ref, key_ref, factor_ref, sum_ref, packet_ref):
    fill_packet(place, chunk, x_ref, key_ref[...], factor_ref[...], sum_ref[...], packet_ref)


def make_ends(place, chunk, *arrays):
    return call(
        functools.partial(ends_kernel, place, chunk), [PACKET], arrays, "ends", 2 * TOK * STATE * WIDTH, kept=range(4)
    )[0]


def merge_kernel(bit, chunk, *refs):
    state_ref = sum_ref = None
    if bit == 0:
        own_ref, got_ref, packet_ref, state_ref, sum_ref = refs
        own_sum = read_total(own_ref[BODY:PACK])
    else:
        own_ref, own_sum_ref, got_ref, packet_ref = refs[:4]
        own_sum = own_sum_ref[0:1]
        if bit < LEVELS - 2:
            state_ref, sum_ref = refs[4:]
    right = position()[bit] == 1
    got_sum = read_total(got_ref[BODY:PACK])
    decay = jnp.broadcast_to(jnp.exp(jnp.where(right, own_sum, got_sum)), (8, 128))
    sums = own_sum + got_sum
    if sum_ref is not None:
        sum_ref[...] = jnp.broadcast_to(sums, (8, 128))
    packet_ref[BODY:PACK] = total_rows(jnp.broadcast_to(sums, (16, 128)))
    for pair in range(PAIRS):
        rows = pl.ds(pair * STATE, STATE)
        own = own_ref[rows].astype(F32)
        got = got_ref[rows].astype(F32)
        factor = spread(decay, 2 * (chunk * PAIRS + pair))[0:1]
        state = jnp.where(right, got, own) * factor + jnp.where(right, own, got)
        if state_ref is not None:
            state_ref[rows] = state
        packet_ref[rows] = state.astype(BF16)


def merge(bit, chunk, *arrays):
    outs = [PACKET] + ([pltpu.VMEM((BODY, 128), F32), SUMS] if bit < LEVELS - 2 else [])
    return call(
        functools.partial(merge_kernel, bit, chunk), outs, arrays, "merge", 1 << 19, 4096, range(len(arrays))
    )


def tables_kernel(decay_ref, mix_ref, key_ref, query_ref, scores_ref, column_ref, row_ref, own_ref, sent_ref):
    bits = position()
    core = bits[0]
    decay = decay_ref[...]
    causal = triangle(lambda r, c: r >= c)
    cum_column = exact_dot(causal, pad_heads(decay), ((1,), (1,)))
    cum_row = cum_column.T[0:HEADS]
    row_ref[...] = cum_row * LOG2E
    mix = jnp.concatenate([mix_ref[0], jnp.ones((128 - HEADS, TOK), F32)], axis=0)
    column_ref[...] = (cum_column + jnp.log(mix).T) * LOG2E
    gate = jnp.exp(cum_row)
    weights = [mix_ref[level + 1] * gate * bits[level].astype(F32) for level in range(LEVELS)]
    unused = [jnp.zeros((128 - SHARE * LEVELS, TOK), F32)]
    low = jnp.concatenate([weight[:SHARE] for weight in weights] + unused, axis=0).T
    high = jnp.concatenate([weight[SHARE:] for weight in weights] + unused, axis=0).T
    own_ref[...] = jnp.where(core == 0, low, high)
    queries = query_ref[...]
    sent_ref[:, 0:128] = queries
    far = jnp.where(core == 0, high, low)
    far_high = far.astype(BF16)
    sent_ref[:, 128:256] = far_high
    sent_ref[:, 256:384] = (far - far_high.astype(F32)).astype(BF16)
    raw = lax.dot_general(queries, key_ref[...], (((1,), (1,)), ((), ())), preferred_element_type=F32)
    scores_ref[...] = raw * causal.astype(F32)


def local_kernel(place, chunk, scores_ref, column_ref, row_ref, x_ref, total_ref):
    core = position()[0]
    half = core if place == 1 else 1 - core
    upper = TOK // 2
    lane = lax.broadcasted_iota(jnp.int32, (TOK, 128), 1)

    def pair_step(pair, _):
        offset = pl.multiple_of(pair * 128, 128)
        x = x_ref[place, :, pl.ds(offset, 128)]
        top = jnp.zeros((upper, 128), F32)
        bottom = jnp.zeros((upper, 128), F32)
        for side in range(2):
            head = half * SHARE + (chunk * PAIRS + pair) * 2 + side
            column = jnp.take_along_axis(column_ref[...], jnp.full((TOK, 128), head, jnp.int32), axis=1)
            row = row_ref[pl.ds(head, 1)]
            chosen = jnp.where((lane < HEAD) == (side == 0), x, jnp.zeros_like(x))
            gap = column[:upper] - row[:, :upper]
            mixing = (scores_ref[:upper, :upper] * jnp.exp2(jnp.minimum(gap, 1.0))).astype(BF16)
            top = top + jnp.dot(mixing, chosen[:upper], preferred_element_type=F32)
            below = column[upper:]
            gap = jnp.concatenate([below, below], axis=1) - row
            mixing = (scores_ref[upper:] * jnp.exp2(jnp.minimum(gap, 1.0))).astype(BF16)
            bottom = bottom + jnp.dot(mixing, chosen, preferred_element_type=F32)
        total_ref[:upper, pl.ds(offset, 128)] = top
        total_ref[upper:, pl.ds(offset, 128)] = bottom
        return 0

    lax.fori_loop(0, PAIRS, pair_step, 0, unroll=True)


def make_local(place, chunk, *arrays):
    return call(
        functools.partial(local_kernel, place, chunk), [PART], arrays, "local", 4 * TOK * TOK * WIDTH,
        2 * PAIRS * TOK * TOK, kept=range(4),
    )[0]


def duo_columns(packet_ref, duo):
    rows = duo * 256
    return jnp.concatenate([packet_ref[rows : rows + 128], packet_ref[rows + 128 : rows + 256]], axis=1)


def duo_spread(table, first):
    return jnp.concatenate([spread(table, first), spread(table, first + 2)], axis=1)


def far_tables(far_ref):
    return far_ref[:, 0:128], far_ref[:, 128:256].astype(F32) + far_ref[:, 256:384].astype(F32)


def level_term(level, chunk, duo, queries, packet_ref, weights, gap):
    product = jnp.dot(queries, duo_columns(packet_ref, duo), preferred_element_type=F32)
    pair = chunk * PAIRS + duo * 2
    return product * (duo_spread(weights, level * SHARE + pair * 2) * duo_spread(gap, pair * 2)[0:1])


def levels_kernel(wanted, chunk, *refs):
    bits = position()
    own, far = (refs[0][...], refs[1][...]), far_tables(refs[2])
    refs = refs[3:]
    if wanted[0] == 0:
        total_ref, kept_ref, *packets = refs[:-4]
        totals = (total_ref, None)
        gaps = [jnp.zeros((8, 128), F32)] * 2
    else:
        totals, gaps, packets = refs[0:2], [refs[2][...], refs[3][...]], refs[4:-4]
        kept_ref = None
    outs, gap_outs = refs[-4:-2], refs[-2:]
    for side in range(2):
        queries, weights = far if side else own
        used = [kept_ref if side == 1 and level == 0 else packet for level, packet in zip(wanted, packets)]
        gap, before = gaps[side], []
        for level, packet in zip(wanted, used):
            before.append(jnp.exp(gap))
            bit = 1 - bits[0] if side == 1 and level == 0 else bits[level]
            gap = gap + read_total(packet[BODY:PACK]) * bit.astype(F32)
        gap_outs[side][...] = gap
        for duo in range(PAIRS // 2):
            lanes = slice(duo * 256, duo * 256 + 256)
            running = None if totals[side] is None else totals[side][:, lanes]
            for level, packet, factor in zip(wanted, used, before):
                term = level_term(level, chunk, duo, queries, packet, weights, factor)
                running = term if running is None else running + term
            outs[side][:, lanes] = running


def add_levels(wanted, chunk, *arrays):
    return call(
        functools.partial(levels_kernel, wanted, chunk), [PART, PART, SUMS, SUMS], arrays, "levels",
        4 * len(wanted) * TOK * STATE * WIDTH, kept=range(len(arrays)),
    )


def last_kernel(far, chunk, duos, *refs):
    if far:
        queries, weights = far_tables(refs[0])
    else:
        queries, weights = refs[0][...], refs[1][...]
    total_ref, gap_ref, packet_ref, out_ref = refs[-4:]
    gap = jnp.exp(gap_ref[...])
    for place, duo in enumerate(duos):
        lanes = slice(duo * 256, duo * 256 + 256)
        term = level_term(LEVELS - 1, chunk, duo, queries, packet_ref, weights, gap)
        out_ref[:, place * 256 : place * 256 + 256] = (total_ref[:, lanes] + term).astype(BF16)


def add_last(far, chunk, *arrays, duos=tuple(range(PAIRS // 2))):
    return call(
        functools.partial(last_kernel, far, chunk, duos), [pltpu.VMEM((TOK, 256 * len(duos)), BF16)], arrays, "last",
        2 * TOK * STATE * WIDTH, kept=range(len(arrays)),
    )[0]


def finish_kernel(first, *refs):
    out_ref, buffer, sems = refs[-3:]
    core = position()[0]
    copies = []

    def send(source, half, chunk, start, width):
        columns = pl.ds(pl.multiple_of(half * (CHUNKS * WIDTH) + chunk * WIDTH + start, 256), width)
        copies.append(pltpu.make_async_copy(source, out_ref.at[:, columns], sems.at[len(copies)]))
        copies[-1].start()

    if first:
        for chunk in range(CHUNKS):
            send(refs[chunk], core, chunk, 0, WIDTH)
        rest_ref, part_refs, chunk = refs[CHUNKS], [refs[CHUNKS + 1]], 0
    else:
        rest_ref, part_refs, chunk = refs[0], refs[1 : 1 + WIDTH // 256], CHUNKS - 1
    for piece in range(WIDTH // 256):
        lanes = slice(piece * 256, piece * 256 + 256)
        part = part_refs[0][:, lanes] if first else part_refs[piece][...]
        buffer[piece] = (rest_ref[:, lanes] + part.astype(F32)).astype(BF16)
        send(buffer.at[piece], 1 - core, chunk, piece * 256, 256)
    for copy in copies:
        copy.wait()


def finish(first, arrays, out=None):
    count = len(arrays)
    return call(
        functools.partial(finish_kernel, first), [jax.ShapeDtypeStruct((TOK, HEADS * HEAD), BF16)],
        [*arrays] if first else [*arrays, out], "finish", TOK * WIDTH, kept=range(count),
        far=() if first else (count,), out_specs=[ANY], aliases=None if first else {count: 0},
        scratch=[pltpu.VMEM((WIDTH // 256, TOK, 256), BF16), pltpu.SemaphoreType.DMA((CHUNKS + WIDTH // 256,))],
    )[0]


def body(inputs, write_keys, read_queries, decay_log, level_mix):
    devices = lax.axis_size("ctx")

    def swap(array, mask, senders=None):
        return lax.ppermute(array, "ctx", [(i, i ^ mask) for i in range(senders or devices)])

    def after(*arrays):
        return lax.optimization_barrier(arrays)

    chunks = range(CHUNKS)
    masks = (1, 2, 6, 8, 24)
    kept, x, got, state, packet = ([None] * CHUNKS for _ in range(5))
    history = [[] for _ in chunks]
    sent, factor, sums, decay, keys, queries, mix, *x = call(
        fetch_kernel,
        [
            PACKET, TABLE, pltpu.VMEM((16, 128), F32), pltpu.VMEM((HEADS, TOK), F32), pltpu.VMEM((TOK, STATE), BF16),
            pltpu.VMEM((TOK, STATE), BF16), pltpu.VMEM((LEVELS + 1, HEADS, TOK), F32),
        ] + [X_PART] * CHUNKS,
        [decay_log, write_keys, read_queries, level_mix, inputs], "fetch", 2 * TOK * STATE * WIDTH, far=range(5),
        scratch=[pltpu.SemaphoreType.DMA((4,)), pltpu.SemaphoreType.DMA((2 * CHUNKS,))],
    )
    got[0] = swap(sent, masks[0])
    for c in chunks[1:]:
        sent = make_ends(0, c, x[c], keys, factor, sums)
        got[c] = swap(sent, masks[0])
    x[0], _ = after(x[0], sent)
    kept[0] = make_ends(1, 0, x[0], keys, factor, sums)

    def advance(level, c):
        if c > 0:
            got[c], _ = after(got[c], packet[c - 1])
            if level == 0:
                x[c], _ = after(x[c], packet[c - 1])
                kept[c] = make_ends(1, c, x[c], keys, factor, sums)
        history[c].append(got[c])
        if level == 0:
            packet[c], *state[c] = merge(0, c, kept[c], got[c])
        else:
            packet[c], *state[c] = merge(level, c, *state[c], got[c])
        got[c] = swap(packet[c], masks[level + 1], devices // 2 if level == 3 and c in (0, 1) else None)

    advance(0, 0)
    queries, mix, _ = after(queries, mix, packet[0])
    scores, column, row, weights, tables = call(
        tables_kernel,
        [
            pltpu.VMEM((TOK, TOK), F32), TABLE, pltpu.VMEM((HEADS, TOK), F32), TABLE, pltpu.VMEM((TOK, 384), BF16),
        ],
        [decay, mix, keys, queries], "tables", 4 * TOK * TOK * STATE, 16384, kept=range(4),
    )
    got[1], tables, scores = after(got[1], tables, scores)
    local = (scores, column, row)
    levels = [None] * CHUNKS

    def add(wanted, c):
        arrays = [*levels[c], *(history[c][level] for level in wanted)]
        levels[c] = add_levels(wanted, c, queries, weights, far, *arrays)

    advance(0, 1)
    tables, _ = after(tables, packet[1])
    far = swap(tables, 1)
    first_0 = make_local(1, 0, *local, x[0])
    first_1 = make_local(1, 1, *local, x[1])
    levels = [[first_0, kept[0]], [first_1, kept[1]]]
    got[0], far, *levels = after(got[0], far, *levels)
    for c in chunks:
        advance(1, c)
    rest = [None] * CHUNKS
    x[0], levels[0], _ = after(x[0], levels[0], packet[1])
    add((0, 1), 0)
    rest[0] = make_local(0, 0, *local, x[0])
    got[0], levels[0], rest[0] = after(got[0], levels[0], rest[0])
    for c in chunks:
        advance(2, c)
    x[1], levels[0], levels[1], _ = after(x[1], *levels, packet[1])
    add((0, 1), 1)
    add((2,), 0)
    rest[1] = make_local(0, 1, *local, x[1])
    got[0], levels[0], levels[1], rest[1] = after(got[0], *levels, rest[1])
    for c in chunks:
        advance(3, c)
    levels[0], levels[1], _ = after(*levels, packet[1])
    add((3,), 0)
    add((2, 3), 1)
    got[0], levels[0], levels[1] = after(got[0], *levels)
    done, parts = [None] * CHUNKS, [None] * CHUNKS
    for c in chunks:
        total, far_total, gap, far_gap = levels[c]
        if c == 0:
            part = add_last(True, c, far, far_total, far_gap, got[c])
            parts[c] = swap(part, 1)
        else:
            parts[c], late = [], got[c]
            for duo in range(PAIRS // 2):
                part = add_last(True, c, far, far_total, far_gap, late, duos=(duo,))
                parts[c].append(swap(part, 1))
                late, _ = after(late, part)
        late, _ = after(got[c], part)
        done[c] = add_last(False, c, queries, weights, total, gap, late)
        if c == 0:
            got[1], done[0] = after(got[1], done[0])
    out = finish(True, [*done, rest[0], parts[0]])
    parts[1], out = after(parts[1], out)
    return finish(False, [rest[1], *parts[1]], out)


def solution(mesh):
    placed = (
        P(("seq", "ctx"), None),
        P(("seq", "ctx"), None),
        P(("seq", "ctx"), None),
        P(None, ("seq", "ctx")),
        P(None, None, ("seq", "ctx")),
    )
    return jax.shard_map(
        body, mesh=mesh, in_specs=placed, out_specs=P(("seq", "ctx"), None), check_vma=False
    )
```

```python
import functools

import jax
import jax.numpy as jnp
from jax import lax
from jax.experimental import pallas as pl
from jax.experimental.pallas import tpu as pltpu
from jax.sharding import PartitionSpec as P

HEADS = 32
HEAD = 64
STATE = 128
TOK = 256
LEVELS = 5
SHARE = HEADS // 2
CHUNKS = 2
PAIRS = SHARE // 2 // CHUNKS
WIDTH = PAIRS * 128
BODY = PAIRS * STATE
PACK = BODY + 16
LOG2E = 1.4426950408889634
F32 = jnp.float32
BF16 = jnp.bfloat16
VMEM = pl.BlockSpec(memory_space=pltpu.VMEM)
ANY = pl.BlockSpec(memory_space=pl.ANY)
KEPT = pltpu.MemorySpace.VMEM
PACKET = pltpu.VMEM((PACK, 128), BF16)
SUMS = pltpu.VMEM((8, 128), F32)
TABLE = pltpu.VMEM((TOK, 128), F32)
PART = pltpu.VMEM((TOK, WIDTH), F32)
X_PART = pltpu.VMEM((2, TOK, WIDTH), BF16)


def split3(value):
    high = value.astype(BF16)
    rest = value - high.astype(F32)
    middle = rest.astype(BF16)
    low = (rest - middle.astype(F32)).astype(BF16)
    return high, middle, low


def exact_dot(zero_one, value, dims, terms=2):
    return sum(
        lax.dot_general(zero_one, part, (dims, ((), ())), preferred_element_type=F32)
        for part in split3(value)[:terms]
    )


def pad_heads(value):
    return jnp.concatenate([value, jnp.zeros((128 - HEADS, value.shape[1]), F32)], axis=0)


def spread(table, first):
    lane = lax.broadcasted_iota(jnp.int32, table.shape, 1)
    return jnp.take_along_axis(table, jnp.where(lane < HEAD, first, first + 1), axis=1)


def triangle(compare):
    rows = lax.broadcasted_iota(jnp.int32, (TOK, TOK), 0)
    columns = lax.broadcasted_iota(jnp.int32, (TOK, TOK), 1)
    return compare(rows, columns).astype(F32).astype(BF16)


def total_rows(sums):
    row = lax.broadcasted_iota(jnp.int32, sums.shape, 0)
    high, middle, low = (part.astype(F32) for part in split3(sums))
    rows = jnp.where(row == 0, high, jnp.where(row == 1, middle, jnp.where(row == 2, low, 0.0)))
    return rows.astype(BF16)


def read_total(rows):
    return jnp.sum(rows.astype(F32), axis=0, keepdims=True)


def position():
    index = lax.axis_index("ctx")
    return [(index >> bit) & 1 for bit in range(LEVELS)]


def call(kernel, outs, arrays, name, flops, exps=0, kept=(), far=(), out_specs=None, scratch=(), aliases=None):
    arrays = list(arrays)
    for place in kept:
        arrays[place] = pltpu.with_memory_space_constraint(arrays[place], KEPT)
    for place in far:
        arrays[place] = pltpu.with_memory_space_constraint(arrays[place], pltpu.MemorySpace.HBM)
    return pl.pallas_call(
        kernel,
        out_shape=outs,
        in_specs=[ANY if place in far else VMEM for place in range(len(arrays))],
        out_specs=out_specs or [VMEM] * len(outs),
        scratch_shapes=list(scratch),
        input_output_aliases=aliases or {},
        compiler_params=pltpu.CompilerParams(vmem_limit_bytes=20 << 20),
        cost_estimate=pl.CostEstimate(flops=flops * 100, bytes_accessed=1 << 10, transcendentals=0),
        name=name,
    )(*arrays)


def fill_packet(place, chunk, x_ref, keys, factor, sums, packet_ref):
    core = position()[0]
    first = (core if place == 1 else 1 - core) * SHARE
    lane = lax.broadcasted_iota(jnp.int32, sums.shape, 1)
    packet_ref[BODY:PACK] = total_rows(jnp.take_along_axis(sums, (lane + first) & 127, axis=1))
    for duo in range(PAIRS // 2):
        pieces = []
        for pair in (2 * duo, 2 * duo + 1):
            x = x_ref[place, :, pair * 128 : pair * 128 + 128].astype(F32)
            pieces.append((x * spread(factor, first + (chunk * PAIRS + pair) * 2)).astype(BF16))
        decayed = jnp.concatenate(pieces, axis=1)
        state = lax.dot_general(keys, decayed, (((0,), (0,)), ((), ())), preferred_element_type=F32)
        packet_ref[duo * 256 : duo * 256 + 128] = state[:, 0:128].astype(BF16)
        packet_ref[duo * 256 + 128 : duo * 256 + 256] = state[:, 128:256].astype(BF16)


def fetch_kernel(*refs):
    sources, sent_ref, factor_ref, sum_ref = refs[0:5], *refs[5:8]
    targets, x_refs, (small, big) = refs[8:12], refs[12 : 12 + CHUNKS], refs[12 + CHUNKS :]
    core = position()[0]
    copies = [
        pltpu.make_async_copy(source, target, small.at[place])
        for place, (source, target) in enumerate(zip(sources, targets))
    ]
    for chunk in range(CHUNKS):
        for place, half in enumerate((1 - core, core)):
            columns = pl.ds(pl.multiple_of(half * (CHUNKS * WIDTH) + chunk * WIDTH, WIDTH), WIDTH)
            copies.append(
                pltpu.make_async_copy(sources[4].at[:, columns], x_refs[chunk].at[place], big.at[2 * chunk + place])
            )
    for place in (0, 4, 1, *range(5, 4 + 2 * CHUNKS), 2, 3):
        copies[place].start()
    later = triangle(lambda r, c: c > r)
    copies[0].wait()
    decay = pad_heads(targets[0][...])
    factor = jnp.exp(exact_dot(later, decay, ((1,), (1,))))
    sums = exact_dot(jnp.ones((16, TOK), BF16), decay, ((1,), (1,)))
    factor_ref[...] = factor
    sum_ref[...] = sums
    copies[1].wait()
    copies[4].wait()
    fill_packet(0, 0, x_refs[0], targets[1][...], factor, sums, sent_ref)
    for copy in copies[2:4] + copies[5:]:
        copy.wait()


def ends_kernel(place, chunk, x_ref, key_ref, factor_ref, sum_ref, packet_ref):
    fill_packet(place, chunk, x_ref, key_ref[...], factor_ref[...], sum_ref[...], packet_ref)


def make_ends(place, chunk, *arrays):
    return call(
        functools.partial(ends_kernel, place, chunk), [PACKET], arrays, "ends", 2 * TOK * STATE * WIDTH, kept=range(4)
    )[0]


def merge_kernel(bit, chunk, *refs):
    state_ref = sum_ref = None
    if bit == 0:
        own_ref, got_ref, packet_ref, state_ref, sum_ref = refs
        own_sum = read_total(own_ref[BODY:PACK])
    else:
        own_ref, own_sum_ref, got_ref, packet_ref = refs[:4]
        own_sum = own_sum_ref[0:1]
        if bit < LEVELS - 2:
            state_ref, sum_ref = refs[4:]
    right = position()[bit] == 1
    got_sum = read_total(got_ref[BODY:PACK])
    decay = jnp.broadcast_to(jnp.exp(jnp.where(right, own_sum, got_sum)), (8, 128))
    sums = own_sum + got_sum
    if sum_ref is not None:
        sum_ref[...] = jnp.broadcast_to(sums, (8, 128))
    packet_ref[BODY:PACK] = total_rows(jnp.broadcast_to(sums, (16, 128)))
    for pair in range(PAIRS):
        rows = pl.ds(pair * STATE, STATE)
        own = own_ref[rows].astype(F32)
        got = got_ref[rows].astype(F32)
        factor = spread(decay, 2 * (chunk * PAIRS + pair))[0:1]
        state = jnp.where(right, got, own) * factor + jnp.where(right, own, got)
        if state_ref is not None:
            state_ref[rows] = state
        packet_ref[rows] = state.astype(BF16)


def merge(bit, chunk, *arrays):
    outs = [PACKET] + ([pltpu.VMEM((BODY, 128), F32), SUMS] if bit < LEVELS - 2 else [])
    return call(
        functools.partial(merge_kernel, bit, chunk), outs, arrays, "merge", 1 << 19, 4096, range(len(arrays))
    )


def tables_kernel(decay_ref, mix_ref, key_ref, query_ref, scores_ref, column_ref, row_ref, own_ref, sent_ref):
    bits = position()
    core = bits[0]
    decay = decay_ref[...]
    causal = triangle(lambda r, c: r >= c)
    cum_column = exact_dot(causal, pad_heads(decay), ((1,), (1,)))
    cum_row = cum_column.T[0:HEADS]
    row_ref[...] = cum_row * LOG2E
    mix = jnp.concatenate([mix_ref[0], jnp.ones((128 - HEADS, TOK), F32)], axis=0)
    column_ref[...] = (cum_column + jnp.log(mix).T) * LOG2E
    gate = jnp.exp(cum_row)
    weights = [mix_ref[level + 1] * gate * bits[level].astype(F32) for level in range(LEVELS)]
    unused = [jnp.zeros((128 - SHARE * LEVELS, TOK), F32)]
    low = jnp.concatenate([weight[:SHARE] for weight in weights] + unused, axis=0).T
    high = jnp.concatenate([weight[SHARE:] for weight in weights] + unused, axis=0).T
    own_ref[...] = jnp.where(core == 0, low, high)
    queries = query_ref[...]
    sent_ref[:, 0:128] = queries
    far = jnp.where(core == 0, high, low)
    far_high = far.astype(BF16)
    sent_ref[:, 128:256] = far_high
    sent_ref[:, 256:384] = (far - far_high.astype(F32)).astype(BF16)
    raw = lax.dot_general(queries, key_ref[...], (((1,), (1,)), ((), ())), preferred_element_type=F32)
    scores_ref[...] = raw * causal.astype(F32)


def local_kernel(place, chunk, scores_ref, column_ref, row_ref, x_ref, total_ref):
    core = position()[0]
    half = core if place == 1 else 1 - core
    upper = TOK // 2
    lane = lax.broadcasted_iota(jnp.int32, (TOK, 128), 1)

    def pair_step(pair, _):
        offset = pl.multiple_of(pair * 128, 128)
        x = x_ref[place, :, pl.ds(offset, 128)]
        top = jnp.zeros((upper, 128), F32)
        bottom = jnp.zeros((upper, 128), F32)
        for side in range(2):
            head = half * SHARE + (chunk * PAIRS + pair) * 2 + side
            column = jnp.take_along_axis(column_ref[...], jnp.full((TOK, 128), head, jnp.int32), axis=1)
            row = row_ref[pl.ds(head, 1)]
            chosen = jnp.where((lane < HEAD) == (side == 0), x, jnp.zeros_like(x))
            gap = column[:upper] - row[:, :upper]
            mixing = (scores_ref[:upper, :upper] * jnp.exp2(jnp.minimum(gap, 1.0))).astype(BF16)
            top = top + jnp.dot(mixing, chosen[:upper], preferred_element_type=F32)
            below = column[upper:]
            gap = jnp.concatenate([below, below], axis=1) - row
            mixing = (scores_ref[upper:] * jnp.exp2(jnp.minimum(gap, 1.0))).astype(BF16)
            bottom = bottom + jnp.dot(mixing, chosen, preferred_element_type=F32)
        total_ref[:upper, pl.ds(offset, 128)] = top
        total_ref[upper:, pl.ds(offset, 128)] = bottom
        return 0

    lax.fori_loop(0, PAIRS, pair_step, 0, unroll=True)


def make_local(place, chunk, *arrays):
    return call(
        functools.partial(local_kernel, place, chunk), [PART], arrays, "local", 4 * TOK * TOK * WIDTH,
        2 * PAIRS * TOK * TOK, kept=range(4),
    )[0]


def duo_columns(packet_ref, duo):
    rows = duo * 256
    return jnp.concatenate([packet_ref[rows : rows + 128], packet_ref[rows + 128 : rows + 256]], axis=1)


def duo_spread(table, first):
    return jnp.concatenate([spread(table, first), spread(table, first + 2)], axis=1)


def far_tables(far_ref):
    return far_ref[:, 0:128], far_ref[:, 128:256].astype(F32) + far_ref[:, 256:384].astype(F32)


def level_term(level, chunk, duo, queries, packet_ref, weights, gap):
    product = jnp.dot(queries, duo_columns(packet_ref, duo), preferred_element_type=F32)
    pair = chunk * PAIRS + duo * 2
    return product * (duo_spread(weights, level * SHARE + pair * 2) * duo_spread(gap, pair * 2)[0:1])


def levels_kernel(wanted, chunk, *refs):
    bits = position()
    own, far = (refs[0][...], refs[1][...]), far_tables(refs[2])
    refs = refs[3:]
    if wanted[0] == 0:
        total_ref, kept_ref, *packets = refs[:-4]
        totals = (total_ref, None)
        gaps = [jnp.zeros((8, 128), F32)] * 2
    else:
        totals, gaps, packets = refs[0:2], [refs[2][...], refs[3][...]], refs[4:-4]
        kept_ref = None
    outs, gap_outs = refs[-4:-2], refs[-2:]
    for side in range(2):
        queries, weights = far if side else own
        used = [kept_ref if side == 1 and level == 0 else packet for level, packet in zip(wanted, packets)]
        gap, before = gaps[side], []
        for level, packet in zip(wanted, used):
            before.append(jnp.exp(gap))
            bit = 1 - bits[0] if side == 1 and level == 0 else bits[level]
            gap = gap + read_total(packet[BODY:PACK]) * bit.astype(F32)
        gap_outs[side][...] = gap
        for duo in range(PAIRS // 2):
            lanes = slice(duo * 256, duo * 256 + 256)
            running = None if totals[side] is None else totals[side][:, lanes]
            for level, packet, factor in zip(wanted, used, before):
                term = level_term(level, chunk, duo, queries, packet, weights, factor)
                running = term if running is None else running + term
            outs[side][:, lanes] = running


def add_levels(wanted, chunk, *arrays):
    return call(
        functools.partial(levels_kernel, wanted, chunk), [PART, PART, SUMS, SUMS], arrays, "levels",
        4 * len(wanted) * TOK * STATE * WIDTH, kept=range(len(arrays)),
    )


def last_kernel(far, chunk, *refs):
    if far:
        queries, weights = far_tables(refs[0])
    else:
        queries, weights = refs[0][...], refs[1][...]
    total_ref, gap_ref, packet_ref, out_ref = refs[-4:]
    gap = jnp.exp(gap_ref[...])
    for duo in range(PAIRS // 2):
        lanes = slice(duo * 256, duo * 256 + 256)
        term = level_term(LEVELS - 1, chunk, duo, queries, packet_ref, weights, gap)
        out_ref[:, lanes] = (total_ref[:, lanes] + term).astype(BF16)


def add_last(far, chunk, *arrays):
    return call(
        functools.partial(last_kernel, far, chunk), [pltpu.VMEM((TOK, WIDTH), BF16)], arrays, "last",
        2 * TOK * STATE * WIDTH, kept=range(len(arrays)),
    )[0]


def finish_kernel(first, *refs):
    out_ref, buffer, sems = refs[-3:]
    core = position()[0]
    copies = []

    def send(source, half, chunk, start, width):
        columns = pl.ds(pl.multiple_of(half * (CHUNKS * WIDTH) + chunk * WIDTH + start, 256), width)
        copies.append(pltpu.make_async_copy(source, out_ref.at[:, columns], sems.at[len(copies)]))
        copies[-1].start()

    if first:
        for chunk in range(CHUNKS):
            send(refs[chunk], core, chunk, 0, WIDTH)
        rest_ref, part_ref, chunk = refs[CHUNKS], refs[CHUNKS + 1], 0
    else:
        rest_ref, part_ref, chunk = refs[0], refs[1], CHUNKS - 1
    for piece in range(WIDTH // 256):
        lanes = slice(piece * 256, piece * 256 + 256)
        buffer[piece] = (rest_ref[:, lanes] + part_ref[:, lanes].astype(F32)).astype(BF16)
        send(buffer.at[piece], 1 - core, chunk, piece * 256, 256)
    for copy in copies:
        copy.wait()


def finish(first, arrays, out=None):
    count = len(arrays)
    return call(
        functools.partial(finish_kernel, first), [jax.ShapeDtypeStruct((TOK, HEADS * HEAD), BF16)],
        [*arrays] if first else [*arrays, out], "finish", TOK * WIDTH, kept=range(count),
        far=() if first else (count,), out_specs=[ANY], aliases=None if first else {count: 0},
        scratch=[pltpu.VMEM((WIDTH // 256, TOK, 256), BF16), pltpu.SemaphoreType.DMA((CHUNKS + WIDTH // 256,))],
    )[0]


def body(inputs, write_keys, read_queries, decay_log, level_mix):
    devices = lax.axis_size("ctx")

    def swap(array, mask, senders=None):
        return lax.ppermute(array, "ctx", [(i, i ^ mask) for i in range(senders or devices)])

    def after(*arrays):
        return lax.optimization_barrier(arrays)

    chunks = range(CHUNKS)
    masks = (1, 2, 6, 8, 24)
    kept, x, got, state, packet = ([None] * CHUNKS for _ in range(5))
    history = [[] for _ in chunks]
    sent, factor, sums, decay, keys, queries, mix, *x = call(
        fetch_kernel,
        [
            PACKET, TABLE, pltpu.VMEM((16, 128), F32), pltpu.VMEM((HEADS, TOK), F32), pltpu.VMEM((TOK, STATE), BF16),
            pltpu.VMEM((TOK, STATE), BF16), pltpu.VMEM((LEVELS + 1, HEADS, TOK), F32),
        ] + [X_PART] * CHUNKS,
        [decay_log, write_keys, read_queries, level_mix, inputs], "fetch", 2 * TOK * STATE * WIDTH, far=range(5),
        scratch=[pltpu.SemaphoreType.DMA((4,)), pltpu.SemaphoreType.DMA((2 * CHUNKS,))],
    )
    got[0] = swap(sent, masks[0])
    for c in chunks[1:]:
        sent = make_ends(0, c, x[c], keys, factor, sums)
        got[c] = swap(sent, masks[0])
    x[0], _ = after(x[0], sent)
    kept[0] = make_ends(1, 0, x[0], keys, factor, sums)

    def advance(level, c):
        if c > 0:
            got[c], _ = after(got[c], packet[c - 1])
            if level == 0:
                x[c], _ = after(x[c], packet[c - 1])
                kept[c] = make_ends(1, c, x[c], keys, factor, sums)
        history[c].append(got[c])
        if level == 0:
            packet[c], *state[c] = merge(0, c, kept[c], got[c])
        else:
            packet[c], *state[c] = merge(level, c, *state[c], got[c])
        got[c] = swap(packet[c], masks[level + 1], devices // 2 if level == 3 and c in (0, 1) else None)

    for c in chunks:
        advance(0, c)
    queries, mix, _ = after(queries, mix, packet[-1])
    scores, column, row, weights, tables = call(
        tables_kernel,
        [
            pltpu.VMEM((TOK, TOK), F32), TABLE, pltpu.VMEM((HEADS, TOK), F32), TABLE, pltpu.VMEM((TOK, 384), BF16),
        ],
        [decay, mix, keys, queries], "tables", 4 * TOK * TOK * STATE, 16384, kept=range(4),
    )
    far = swap(tables, 1)
    local = (scores, column, row)
    levels = [None] * CHUNKS

    def add(wanted, c):
        arrays = [*levels[c], *(history[c][level] for level in wanted)]
        levels[c] = add_levels(wanted, c, queries, weights, far, *arrays)

    for c in chunks:
        levels[c] = [make_local(1, c, *local, x[c]), kept[c]]
    got[0], far, *levels = after(got[0], far, *levels)
    for c in chunks:
        advance(1, c)
    rest = [None] * CHUNKS
    x[0], levels[0], _ = after(x[0], levels[0], packet[1])
    add((0, 1), 0)
    rest[0] = make_local(0, 0, *local, x[0])
    got[0], levels[0], rest[0] = after(got[0], levels[0], rest[0])
    for c in chunks:
        advance(2, c)
    x[1], levels[0], levels[1], _ = after(x[1], *levels, packet[1])
    add((0, 1), 1)
    add((2,), 0)
    rest[1] = make_local(0, 1, *local, x[1])
    got[0], levels[0], levels[1], rest[1] = after(got[0], *levels, rest[1])
    for c in chunks:
        advance(3, c)
    levels[0], levels[1], _ = after(*levels, packet[1])
    add((3,), 0)
    add((2, 3), 1)
    got[0], levels[0], levels[1] = after(got[0], *levels)
    done, parts = [None] * CHUNKS, [None] * CHUNKS
    for c in chunks:
        total, far_total, gap, far_gap = levels[c]
        part = add_last(True, c, far, far_total, far_gap, got[c])
        parts[c] = swap(part, 1)
        late, _ = after(got[c], part)
        done[c] = add_last(False, c, queries, weights, total, gap, late)
        if c == 0:
            got[1], done[0] = after(got[1], done[0])
    out = finish(True, [*done, rest[0], parts[0]])
    parts[1], out = after(parts[1], out)
    return finish(False, [rest[1], parts[1]], out)


def solution(mesh):
    placed = (
        P(("seq", "ctx"), None),
        P(("seq", "ctx"), None),
        P(("seq", "ctx"), None),
        P(None, ("seq", "ctx")),
        P(None, None, ("seq", "ctx")),
    )
    return jax.shard_map(
        body, mesh=mesh, in_specs=placed, out_specs=P(("seq", "ctx"), None), check_vma=False
    )
```
